32 devices in a mesh: grp: 1, seq: 8 (over z, y), head: 4 (over x, core).
Axes of the slice: x: 2, y: 2, z: 4, core: 2. Of those that a mesh axis runs over, the one named last changes fastest.
Arguments:
- ssm_values: bfloat16 [2048, 4096], P(('grp', 'seq'), 'head'), may hold values from -6 to 6
- ssm_gate: bfloat16 [2048, 4096], P(('grp', 'seq'), 'head'), may hold values from -6 to 6
- write_proj: bfloat16 [2048, 1024], P(('grp', 'seq'), 'head'), may hold values from -2.5 to 2.5
- read_proj: bfloat16 [2048, 1024], P(('grp', 'seq'), 'head'), may hold values from -2.5 to 2.5
- step_size: float32 [2048, 64], P(('grp', 'seq'), 'head'), may hold values from 0.003125 to 0.2
- decay_power: int32 [64], P('head'), may hold values from 0 to 15
- skip_gain: float32 [64], P('head'), may hold values from 0.5 to 1.5
- norm_gain: float32 [4096], P('head'), may hold values from 0.1 to 1.9
- out_weight: bfloat16 [4096, 2688], P('head', 'seq'), may hold values from -0.09375 to 0.09375
- residual: bfloat16 [2048, 2688], P(('grp', 'seq', 'head')), may hold values from -6 to 6
- expert_norm: float32 [2688], replicated, may hold values from 0.1 to 1.9
- router_weight: bfloat16 [2688, 16], replicated, may hold values from -0.125 to 0.125
- expert_index: int32 [2048, 6], P(('grp', 'seq', 'head')), may hold values from 0 to 15, all different within a row; in each aligned block of 64 rows (0 to 63, 64 to 127, ...) at most 32 rows name the same one
- up_weight: bfloat16 [32, 2688, 928], P(('seq', 'head')), may hold values from -0.125 to 0.125
- down_weight: bfloat16 [32, 928, 2688], P(('seq', 'head')), may hold values from -0.125 to 0.125
Outputs:
- layer_out: bfloat16 [2048, 2688], P(('grp', 'seq', 'head'))
The draws below stay inside these ranges and needn't reach their ends.
Inputs may be any that keep to these rules, and one draw needn't show every extreme that they name: `expert_index`: each row names 6 different experts. In the rows of one device (aligned blocks of 64 rows) no expert is named more than 32 times, a bound that some block reaches.
All inputs are finite; a program needn't handle non-finite values.
Results may differ from the reference program's by a relative error of at most 0.019.
Values may be sent and summed in bfloat16 or wider, within the bound.
A program may use at most 64 MiB of HBM per device.

```python
import math
import jax
import jax.numpy as jnp
import numpy as np
from jax import lax

D = 2688
FF = 1856
HEADS = 64
HEAD_DIM = 64
STATE = 128
GROUPS = 8
TOP = 6
BLOCK_LEN = 256
TOK_DEV = 256
TOKENS = 2048
EXPERTS = 16
CAP = 32
N_HEAD = 4


def draw_step_size(key, part):
    base_key = jax.random.fold_in(key, 11)
    factor_key = jax.random.fold_in(key, 23)
    base = jnp.exp(jax.random.uniform(base_key, (TOKENS, HEADS), jnp.float32, math.log(0.0125), math.log(0.05)))
    shards = TOKENS // TOK_DEV
    factor = jnp.exp(jax.random.uniform(factor_key, (shards, 1, HEADS), jnp.float32, math.log(0.25), math.log(4.0)))
    return (base.reshape(shards, TOK_DEV, HEADS) * factor).reshape(TOKENS, HEADS)


def set_ends(values, stream_key, smallest, top_value):
    index_at = [jax.random.randint(jax.random.fold_in(stream_key, axis), (), 0, length) for axis, length in enumerate(values.shape)]
    longest = values.shape.index(max(values.shape))
    beside = index_at[:longest] + [(index_at[longest] + 1) % values.shape[longest]] + index_at[longest + 1:]
    return values.at[tuple(index_at)].set(smallest).at[tuple(beside)].set(top_value)


def levels(own_key, dims, split, least, top_value):
    loudness = 1.0
    for axis_at, parts in split:
        steps = jax.random.uniform(jax.random.fold_in(jax.random.fold_in(own_key, 6), axis_at), (parts,), jnp.float32, least / len(split), top_value / len(split))
        loudness = loudness * jnp.repeat(jnp.exp(steps), dims[axis_at] // parts).reshape((-1,) + (1,) * (len(dims) - 1 - axis_at))
    return loudness


def assign_block(key, own, number, rows, amount, top, reach, slope):
    order = jax.random.permutation(key, amount)
    crowded, common = load_shares(amount, rows * top, reach, slope, True), load_shares(amount, rows * top, reach, slope, False)
    places = jnp.arange(amount)

    def named(sizes, rotation):
        used = int((sizes > 0).sum())
        fixed = max(1, used // 4)
        shifted = fixed + (places - fixed + rotation * (used - fixed)) % max(1, amount - fixed)
        return jnp.zeros((amount,), jnp.int32).at[order[jnp.where(places < fixed, places, shifted)]].set(jnp.asarray(sizes, jnp.int32))

    sizes = jnp.where(number % 4 == 0, named(crowded, number // 4), named(common, number - number // 4 - 1))
    mixed = jax.random.permutation(jax.random.fold_in(own, 3), amount)
    giver, receiver = mixed[0:amount // 2 * 2:2], mixed[1:amount // 2 * 2:2]
    margin = jnp.minimum(sizes[giver] - 1, reach - sizes[receiver]) // 2
    margin = jnp.where((giver == order[0]) | (receiver == order[0]) | (sizes[receiver] == 0), 0, jnp.maximum(margin, 0))
    shifted = jax.random.randint(jax.random.fold_in(own, 4), (amount // 2,), 0, 1 << 20) % (margin + 1)
    sizes = sizes.at[giver].add(-shifted).at[receiver].add(shifted)
    items = jnp.searchsorted(jnp.cumsum(sizes), jnp.arange(rows * top), side="right").astype(jnp.int32)
    table = items.reshape(top, rows).T
    table = table[jax.random.permutation(jax.random.fold_in(own, 1), rows)]
    rotation = jax.random.randint(jax.random.fold_in(own, 2), (rows, 1), 0, top)
    return jnp.take_along_axis(table, (jnp.arange(top)[None, :] + rotation) % top, axis=1)


def load_shares(number_of, total, reach, skew, full):
    weights = [(1 << 20) // math.isqrt(rank ** skew) + 1 for rank in range(1, number_of + 1)]
    largest = reach if full else min(reach, max(-(-total // number_of), total * weights[0] // sum(weights)))
    least = 1 if total - largest >= number_of - 1 else 0
    holding, spare = [largest] + [least] * (number_of - 1), total - largest - least * (number_of - 1)
    while spare > 0:
        movable = [i for i in range(1, number_of) if holding[i] < largest] or [i for i in range(1, number_of) if holding[i] < reach]
        mass, left = sum([weights[i] for i in movable]), spare
        for i in movable:
            extra = min(reach - holding[i], max(1, left * weights[i] // mass), spare)
            holding[i] = holding[i] + extra
            spare = spare - extra
    return np.array(holding)


def normal_values(stream_key, dims, scale, limit, cuts=(), kind=jnp.bfloat16):
    level = levels(stream_key, dims, cuts, -0.22, 0.18) if cuts else 1.0
    values = jax.random.normal(stream_key, dims, jnp.float32) * scale * level
    return jnp.minimum(jnp.maximum(values, -limit), limit).astype(kind)


def setup_inputs(seed: int = 0, part: int = 0) -> dict:
    seeds = jax.random.split(jax.random.key(seed), 16)
    own_keys = jax.random.split(jax.random.fold_in(seeds[15], part), 16)
    ssm_values = normal_values(own_keys[0], (TOKENS, HEADS * HEAD_DIM), 1.0, 6.0, ((0, 8), (1, 4)))
    ssm_gate = normal_values(own_keys[1], (TOKENS, HEADS * HEAD_DIM), 1.0, 6.0, ((0, 8), (1, 4)))
    write_proj = normal_values(own_keys[2], (TOKENS, GROUPS * STATE), 0.35, 2.5, ((0, 8), (1, 4)))
    read_proj = normal_values(own_keys[3], (TOKENS, GROUPS * STATE), 0.35, 2.5, ((0, 8), (1, 4)))
    step_size = draw_step_size(jax.random.fold_in(jax.random.fold_in(seeds[15], part), 71), part)
    decay_power = set_ends(jax.random.randint(seeds[5], (HEADS,), 0, 16), jax.random.fold_in(seeds[5], 1), 0, 15).astype(jnp.int32)
    skip_gain = jnp.clip(0.5 + 1.0 * jax.random.uniform(seeds[6], (HEADS,), jnp.float32) ** levels(seeds[6], (HEADS,), ((0, 4),), -0.2, 0.2), 0.5, 1.5)
    norm_gain = jnp.clip(1.0 + 0.18 * jax.random.normal(seeds[7], (HEADS * HEAD_DIM,), jnp.float32), 0.1, 1.9)
    out_weight = normal_values(seeds[8], (HEADS * HEAD_DIM, D), (HEADS * HEAD_DIM) ** -0.5, 0.09375, ((0, 4), (1, 8)))
    residual = normal_values(own_keys[9], (TOKENS, D), 1.0, 6.0, ((0, 32),))
    expert_norm = jnp.clip(1.0 + 0.18 * jax.random.normal(seeds[10], (D,), jnp.float32), 0.1, 1.9)
    router_weight = normal_values(seeds[11], (D, EXPERTS), D ** -0.5, 0.125)
    expert_index_keys = jax.random.split(jax.random.fold_in(own_keys[12], 1), TOKENS // (TOK_DEV // N_HEAD))
    expert_index_turns = jax.random.permutation(jax.random.fold_in(own_keys[12], 3), TOKENS // (TOK_DEV // N_HEAD))
    expert_index = jax.vmap(lambda own, number: assign_block(jax.random.fold_in(own_keys[12], 2), own, number, TOK_DEV // N_HEAD, EXPERTS, TOP, CAP, 2))(expert_index_keys, expert_index_turns).reshape((TOKENS, TOP))
    up_weight = normal_values(seeds[13], (2 * EXPERTS, D, FF // 2), D ** -0.5, 0.125, ((0, 32),))
    down_weight = normal_values(seeds[14], (2 * EXPERTS, FF // 2, D), FF ** -0.5, 0.125, ((0, 32),))
    return {"ssm_values": ssm_values, "ssm_gate": ssm_gate, "write_proj": write_proj, "read_proj": read_proj, "step_size": step_size, "decay_power": decay_power, "skip_gain": skip_gain, "norm_gain": norm_gain, "out_weight": out_weight, "residual": residual, "expert_norm": expert_norm, "router_weight": router_weight, "expert_index": expert_index, "up_weight": up_weight, "down_weight": down_weight}


EPSILON = 1e-05
ROUTE_SCALE = 2.5

def rounded(value):
    return lax.optimization_barrier(value.astype(jnp.bfloat16)).astype(jnp.float32)

def reference(ssm_values, ssm_gate, write_proj, read_proj, step_size, decay_power, skip_gain, norm_gain, out_weight, residual, expert_norm, router_weight, expert_index, up_weight, down_weight):
    per_group = HEADS // GROUPS
    decay_rates = jnp.exp2(-decay_power.astype(jnp.float32))
    blocks = TOKENS // BLOCK_LEN
    block_values = ssm_values.reshape(blocks, BLOCK_LEN, HEADS, HEAD_DIM)
    block_steps = step_size.reshape(blocks, BLOCK_LEN, HEADS)
    block_write = write_proj.reshape(blocks, BLOCK_LEN, GROUPS, STATE)
    block_read = read_proj.reshape(blocks, BLOCK_LEN, GROUPS, STATE)
    causal = jnp.tril(jnp.ones((BLOCK_LEN, BLOCK_LEN), dtype=bool))

    def advance(carry_state, pieces):
        values_in, steps_in, write_in, read_in = pieces
        log_decay = -steps_in * decay_rates[None, :]
        cumulative = jnp.cumsum(log_decay, axis=0)
        scores = jnp.einsum('tgn,sgn->gts', read_in.astype(jnp.float32), write_in.astype(jnp.float32))
        scores = jnp.repeat(scores, per_group, axis=0)
        decays = jnp.exp(cumulative.T[:, :, None] - cumulative.T[:, None, :])
        mixing = rounded(jnp.where(causal[None], scores * decays * steps_in.T[:, None, :], 0.0))
        inner_out = jnp.einsum('hts,shp->thp', mixing, values_in.astype(jnp.float32))
        block_total = cumulative[-1]
        weighted = rounded(values_in.astype(jnp.float32) * (jnp.exp(block_total[None, :] - cumulative) * steps_in)[:, :, None])
        write_heads = jnp.repeat(write_in, per_group, axis=1).astype(jnp.float32)
        read_heads = jnp.repeat(read_in, per_group, axis=1).astype(jnp.float32)
        fresh_state = jnp.einsum('shp,shn->hpn', weighted, write_heads)
        carried = jnp.einsum('thn,hpn->thp', read_heads, rounded(carry_state)) * jnp.exp(cumulative)[:, :, None]
        new_state = jnp.exp(block_total)[:, None, None] * carry_state + fresh_state
        return (new_state, inner_out + carried)
    zero_state = jnp.zeros((HEADS, HEAD_DIM, STATE), jnp.float32)
    final_state, outputs = lax.scan(advance, zero_state, (block_values, block_steps, block_write, block_read))
    values_all = ssm_values.reshape(TOKENS, HEADS, HEAD_DIM).astype(jnp.float32)
    ssm_out = outputs.reshape(TOKENS, HEADS, HEAD_DIM) + skip_gain[None, :, None] * values_all
    gate_vals = ssm_gate.reshape(TOKENS, HEADS, HEAD_DIM).astype(jnp.float32)
    gated = (ssm_out * jax.nn.silu(gate_vals)).reshape(TOKENS, GROUPS, per_group * HEAD_DIM)
    inv_rms = lax.rsqrt(lax.optimization_barrier(jnp.mean(gated * gated, axis=-1, keepdims=True)) + EPSILON)
    normed = ((gated * inv_rms).reshape(TOKENS, HEADS * HEAD_DIM) * norm_gain[None, :]).astype(jnp.bfloat16)
    mixed_out = jnp.dot(normed, out_weight, preferred_element_type=jnp.float32)
    hidden = residual.astype(jnp.float32) + mixed_out
    inputs = (hidden * lax.rsqrt(lax.optimization_barrier(jnp.mean(hidden * hidden, axis=-1, keepdims=True)) + EPSILON) * expert_norm[None, :]).astype(jnp.bfloat16)
    logits = jnp.dot(inputs, router_weight, preferred_element_type=jnp.float32)
    picked = jnp.take_along_axis(logits, expert_index, axis=1)
    probability = jax.nn.sigmoid(picked)
    shares = ROUTE_SCALE * probability / lax.optimization_barrier(jnp.sum(probability, axis=1, keepdims=True))
    rows_dev = TOK_DEV // N_HEAD
    count_blocks = TOKENS // rows_dev
    expert_hits = (expert_index[:, :, None] == jnp.arange(EXPERTS, dtype=jnp.int32)[None, None, :]).astype(jnp.int32)
    flat_hits = expert_hits.reshape(count_blocks, rows_dev * TOP, EXPERTS)
    before = jnp.cumsum(flat_hits, axis=1) - flat_hits
    slot_index = lax.optimization_barrier(jnp.sum(before * flat_hits, axis=-1)).reshape(TOKENS * TOP)
    expert_flat = expert_index.reshape(TOKENS * TOP)
    token_ids = jnp.repeat(jnp.arange(TOKENS, dtype=jnp.int32), TOP)
    column = token_ids // rows_dev * CAP + slot_index
    row_table = jnp.full((EXPERTS, count_blocks * CAP), TOKENS, jnp.int32).at[expert_flat, column].set(token_ids)
    share_table = jnp.zeros((EXPERTS, count_blocks * CAP), jnp.float32).at[expert_flat, column].set(shares.reshape(TOKENS * TOP))
    padded = jnp.concatenate([inputs, jnp.zeros((1, D), jnp.bfloat16)], axis=0)
    up_pairs = up_weight.reshape(EXPERTS, 2, D, FF // 2)
    down_pairs = down_weight.reshape(EXPERTS, 2, FF // 2, D)

    def expert(totals, pieces):
        up_pair, down_pair, row_ids, share_row = pieces
        chosen = padded[row_ids]
        half_outs = []
        for half_index in range(2):
            activation = jnp.dot(chosen, up_pair[half_index], preferred_element_type=jnp.float32)
            activation = jnp.maximum(activation, 0.0)
            activation = (activation * activation).astype(jnp.bfloat16)
            half_outs.append(rounded(jnp.dot(activation, down_pair[half_index], preferred_element_type=jnp.float32)))
        result = rounded(half_outs[0] + half_outs[1])
        totals = totals.at[row_ids].add(share_row[:, None] * result)
        return (totals, None)
    initial = jnp.zeros((TOKENS + 1, D), jnp.float32)
    totals, unused = lax.scan(expert, initial, (up_pairs, down_pairs, row_table, share_table))
    return (hidden + totals[:TOKENS]).astype(jnp.bfloat16)
```

```python
import jax
import jax.numpy as jnp
from jax import lax
from jax.sharding import PartitionSpec as P

HEADS = 64
HEAD_DIM = 64
STATE = 128
GROUPS = 8
TOP = 6
BLOCK_LEN = 256


EPSILON = 1e-05
ROUTE_SCALE = 2.5


def shift(x, axis, step):
    size = lax.axis_size(axis)
    pairs = [(i, i + step) for i in range(size) if 0 <= i + step < size]
    return lax.ppermute(x, axis, pairs)


def entering(decay, state):
    count = lax.axis_size("seq") // 2
    odd = lax.axis_index("seq") % 2 == 1
    heads, rows, width = state.shape

    def pack(decay, state):
        tail = jnp.broadcast_to(decay[:, None, None], (heads, 8, width))
        return jnp.concatenate([state, tail], axis=1).astype(jnp.bfloat16)

    def unpack(packed):
        wide = packed.astype(jnp.float32)
        return wide[:, rows, 0], wide[:, :rows]

    def combine(earlier, later):
        return (earlier[0] * later[0], later[0][:, None, None] * earlier[1] + later[1])

    mine = (decay, state)
    other = unpack(partner(pack(*mine), "seq", 0))
    first = jax.tree.map(lambda a, b: jnp.where(odd, a, b), other, mine)
    second = jax.tree.map(lambda a, b: jnp.where(odd, a, b), mine, other)
    before = jax.tree.map(lambda a: jnp.where(odd, a, jnp.zeros_like(a)), other)
    before = (jnp.where(odd, before[0], 1.0), before[1])
    pair = combine(first, second)
    reach, scan = 1, unpack(shift(pack(*pair), "seq", 2))
    while reach < count - 1:
        scan = combine(unpack(shift(pack(*scan), "seq", 2 * reach)), scan)
        reach *= 2
    return combine(scan, before)[1]


def gather_columns(block):
    count = lax.axis_size("seq") // 2
    place = lax.axis_index("seq") // 2
    up, down = [block], [block]
    for step in range(1, count):
        up.append(shift(up[-1], "seq", 2))
        down.append(shift(down[-1], "seq", -2))
    slots = [block]
    for step in range(1, count):
        slots.append(jnp.where(place + step < count, down[step], up[count - step]))
    return [(slot, partner(slot, "seq", 0)) for slot in slots]


def project(normed, slots):
    count = len(slots)
    place, odd = lax.axis_index("seq") // 2, lax.axis_index("seq") % 2 == 1
    parts = []
    for pair in slots:
        first, second = (
            jnp.dot(normed, block, preferred_element_type=jnp.float32).astype(jnp.bfloat16)
            for block in pair
        )
        parts.append(
            jnp.concatenate(
                [jnp.where(odd, second, first), jnp.where(odd, first, second)], axis=1
            )
        )
    parts = jnp.stack(parts + parts[:-1])
    parts = lax.dynamic_slice_in_dim(parts, (count - place) % count, count, axis=0)
    return parts.transpose(1, 0, 2).reshape(normed.shape[0], -1)


def sum_rows(x, axis):
    size = lax.axis_size(axis)
    bits = size.bit_length() - 1
    width = x.shape[-1]
    x = x.reshape((2,) * bits + (-1, width))
    for bit in range(bits):
        mine = lax.axis_index(axis) >> bit & 1
        where = bits - 1 - bit
        keep = lax.dynamic_index_in_dim(x, mine, where, keepdims=False)
        give = lax.dynamic_index_in_dim(x, 1 - mine, where, keepdims=False)
        got = partner(give.astype(jnp.bfloat16), axis, bit)
        x = keep.astype(jnp.float32) + got.astype(jnp.float32)
    return x


def partner(x, axis, stride):
    return lax.ppermute(x, axis, [(i, i ^ 1 << stride) for i in range(lax.axis_size(axis))])


def expert_half(slot_rows, up_weight, down_weight):
    model_width = slot_rows.shape[-1]
    flat_rows = slot_rows.reshape(-1, model_width)
    activation = jnp.dot(flat_rows, up_weight[0], preferred_element_type=jnp.float32)
    activation = jnp.maximum(activation, 0.0)
    activation = (activation * activation).astype(jnp.bfloat16)
    output = jnp.dot(activation, down_weight[0], preferred_element_type=jnp.float32).astype(
        jnp.bfloat16
    )
    return output.reshape(slot_rows.shape)


def per_device(
    ssm_values,
    ssm_gate,
    write_proj,
    read_proj,
    step_size,
    decay_power,
    skip_gain,
    norm_gain,
    out_weight,
    residual,
    expert_norm,
    router_weight,
    expert_index,
    up_weight,
    down_weight,
):
    slots = gather_columns(out_weight)
    tokens_dev = ssm_values.shape[0]
    heads_dev = step_size.shape[1]
    per_group = HEADS // GROUPS
    groups_dev = heads_dev // per_group
    count_blocks = tokens_dev // BLOCK_LEN
    decay_rates = jnp.exp2(-decay_power.astype(jnp.float32))
    values = ssm_values.reshape(count_blocks, BLOCK_LEN, heads_dev, HEAD_DIM)
    steps_all = step_size.reshape(count_blocks, BLOCK_LEN, heads_dev)
    writes = write_proj.reshape(count_blocks, BLOCK_LEN, groups_dev, STATE)
    reads = read_proj.reshape(count_blocks, BLOCK_LEN, groups_dev, STATE)
    causal = jnp.tril(jnp.ones((BLOCK_LEN, BLOCK_LEN), dtype=bool))

    def one_block(pieces):
        values_in, steps_in, write_in, read_in = pieces
        log_decay = -steps_in * decay_rates[None, :]
        cumulative = jnp.cumsum(log_decay, axis=0)
        scores = jnp.einsum("tgn,sgn->gts", read_in, write_in, preferred_element_type=jnp.float32)
        scores = jnp.repeat(scores, per_group, axis=0)
        decays = jnp.exp(cumulative.T[:, :, None] - cumulative.T[:, None, :])
        mixing = jnp.where(causal[None], scores * decays * steps_in.T[:, None, :], 0.0).astype(
            jnp.bfloat16
        )
        inner_out = jnp.einsum(
            "hts,shp->thp", mixing, values_in, preferred_element_type=jnp.float32
        )
        block_total = cumulative[-1]
        weighted = (
            values_in.astype(jnp.float32)
            * (jnp.exp(block_total[None, :] - cumulative) * steps_in)[:, :, None]
        ).astype(jnp.bfloat16)
        write_heads = jnp.repeat(write_in, per_group, axis=1)
        fresh_state = jnp.einsum(
            "shp,shn->hpn", weighted, write_heads, preferred_element_type=jnp.float32
        )
        return (inner_out, fresh_state, block_total, cumulative)

    inner_all, fresh_all, totals_blk, cumul_all = lax.map(
        one_block, (values, steps_all, writes, reads)
    )

    def summarize(carried_in, pieces):
        decay_prod, summary = carried_in
        block_total, fresh_state = pieces
        factor = jnp.exp(block_total)
        return ((decay_prod * factor, factor[:, None, None] * summary + fresh_state), None)

    zero_state = jnp.zeros((heads_dev, HEAD_DIM, STATE), jnp.float32)
    (device_decay, device_state), unused = lax.scan(
        summarize, (jnp.ones((heads_dev,), jnp.float32), zero_state), (totals_blk, fresh_all)
    )

    incoming = entering(device_decay, device_state)

    def emit_rows(carry_state, pieces):
        read_in, cumulative, block_total, fresh_state = pieces
        read_heads = jnp.repeat(read_in, per_group, axis=1)
        carried = jnp.einsum(
            "thn,hpn->thp",
            read_heads,
            carry_state.astype(jnp.bfloat16),
            preferred_element_type=jnp.float32,
        )
        carried = carried * jnp.exp(cumulative)[:, :, None]
        return (jnp.exp(block_total)[:, None, None] * carry_state + fresh_state, carried)

    final_state, carried_all = lax.scan(
        emit_rows, incoming, (reads, cumul_all, totals_blk, fresh_all)
    )
    values_flat = ssm_values.reshape(tokens_dev, heads_dev, HEAD_DIM).astype(jnp.float32)
    ssm_out = (inner_all + carried_all).reshape(tokens_dev, heads_dev, HEAD_DIM) + skip_gain[
        None, :, None
    ] * values_flat
    gate_vals = ssm_gate.reshape(tokens_dev, heads_dev, HEAD_DIM).astype(jnp.float32)
    gated = (ssm_out * jax.nn.silu(gate_vals)).reshape(tokens_dev, groups_dev, per_group * HEAD_DIM)
    inv_rms = lax.rsqrt(jnp.mean(gated * gated, axis=-1, keepdims=True) + EPSILON)
    normed = (
        (gated * inv_rms).reshape(tokens_dev, heads_dev * HEAD_DIM) * norm_gain[None, :]
    ).astype(jnp.bfloat16)
    rows_own = tokens_dev // lax.axis_size("head")
    mixed_out = sum_rows(project(normed, slots), "head")
    hidden = residual.astype(jnp.float32) + mixed_out
    inputs = (
        hidden
        * lax.rsqrt(jnp.mean(hidden * hidden, axis=-1, keepdims=True) + EPSILON)
        * expert_norm[None, :]
    ).astype(jnp.bfloat16)
    logits = jnp.dot(inputs, router_weight, preferred_element_type=jnp.float32)
    experts = router_weight.shape[1]
    model_width = inputs.shape[1]
    expert_hits = expert_index[:, :, None] == jnp.arange(experts, dtype=jnp.int32)[None, None, :]
    picked = jnp.sum(jnp.where(expert_hits, logits[:, None, :], 0.0), axis=-1)
    probability = jax.nn.sigmoid(picked)
    shares = ROUTE_SCALE * probability / jnp.sum(probability, axis=1, keepdims=True)
    capacity = (
        8
        * TOP
        * tokens_dev
        // (3 * lax.axis_size("seq") * lax.axis_size("head") * lax.axis_size("head"))
    )
    flat_hits = expert_hits.astype(jnp.int32).reshape(rows_own * TOP, experts)
    before = jnp.cumsum(flat_hits, axis=0) - flat_hits
    slot_index = jnp.sum(before * flat_hits, axis=1)
    target = expert_index.reshape(rows_own * TOP) * capacity + slot_index
    placing = jnp.arange(experts * capacity, dtype=jnp.int32)[:, None] == target[None, :]
    placing = jnp.any(placing.reshape(experts * capacity, rows_own, TOP), axis=2).astype(
        jnp.bfloat16
    )
    outgoing = jnp.dot(placing, inputs, preferred_element_type=jnp.float32).astype(jnp.bfloat16)
    outgoing = outgoing.reshape(experts, capacity, model_width)
    halves = outgoing.reshape(experts, 2, capacity // 2, model_width).reshape(
        2 * experts, capacity // 2, model_width
    )
    slot_rows = lax.all_to_all(halves, ("seq", "head"), split_axis=0, concat_axis=0, tiled=True)
    other_rows = partner(slot_rows, "head", 0)
    both_rows = jnp.concatenate([slot_rows, other_rows], axis=1)
    both_parts = expert_half(both_rows, up_weight, down_weight)
    own_part = both_parts[:, : slot_rows.shape[1]]
    other_part = both_parts[:, slot_rows.shape[1] :]
    back_part = partner(other_part, "head", 0)
    summed = (own_part.astype(jnp.float32) + back_part.astype(jnp.float32)).astype(jnp.bfloat16)
    returned = lax.all_to_all(summed, ("seq", "head"), split_axis=0, concat_axis=0, tiled=True)
    results = returned.reshape(experts, 2, capacity // 2, model_width).reshape(
        experts, capacity, model_width
    )
    gathered = results.reshape(experts * capacity, model_width)[target].reshape(
        rows_own, TOP, model_width
    )
    moe_out = jnp.sum(shares[:, :, None] * gathered.astype(jnp.float32), axis=1)
    return (hidden + moe_out).astype(jnp.bfloat16)


def solution(mesh):
    return jax.shard_map(
        per_device,
        mesh=mesh,
        in_specs=(
            P(("grp", "seq"), "head"),
            P(("grp", "seq"), "head"),
            P(("grp", "seq"), "head"),
            P(("grp", "seq"), "head"),
            P(("grp", "seq"), "head"),
            P("head"),
            P("head"),
            P("head"),
            P("head", "seq"),
            P(("grp", "seq", "head"), None),
            P(),
            P(),
            P(("grp", "seq", "head"), None),
            P(("seq", "head"), None, None),
            P(("seq", "head"), None, None),
        ),
        out_specs=P(("grp", "seq", "head"), None),
        check_vma=False,
    )
```

```python
import functools
import jax
import jax.numpy as jnp
from jax import lax
from jax.experimental import pallas as pl
from jax.experimental.pallas import tpu as pltpu
from jax.sharding import PartitionSpec as P

HEADS = 64
HEAD_DIM = 64
STATE = 128
GROUPS = 8
TOP = 6
BLOCK_LEN = 256


EPSILON = 1e-05
ROUTE_SCALE = 2.5


def shift(x, axis, step):
    size = lax.axis_size(axis)
    pairs = [(i, i + step) for i in range(size) if 0 <= i + step < size]
    return lax.ppermute(x, axis, pairs)


def entering(decay, state):
    count = lax.axis_size("seq") // 2
    odd = lax.axis_index("seq") % 2 == 1
    heads, rows, width = state.shape

    def pack(decay, state):
        tail = jnp.broadcast_to(decay[:, None, None], (heads, 8, width))
        return jnp.concatenate([state, tail], axis=1).astype(jnp.bfloat16)

    def unpack(packed):
        wide = packed.astype(jnp.float32)
        return wide[:, rows, 0], wide[:, :rows]

    def combine(earlier, later):
        return (earlier[0] * later[0], later[0][:, None, None] * earlier[1] + later[1])

    mine = (decay, state)
    other = unpack(partner(pack(*mine), "seq", 0))
    first = jax.tree.map(lambda a, b: jnp.where(odd, a, b), other, mine)
    second = jax.tree.map(lambda a, b: jnp.where(odd, a, b), mine, other)
    before = jax.tree.map(lambda a: jnp.where(odd, a, jnp.zeros_like(a)), other)
    before = (jnp.where(odd, before[0], 1.0), before[1])
    pair = combine(first, second)
    reach, scan = 1, unpack(shift(pack(*pair), "seq", 2))
    while reach < count - 1:
        scan = combine(unpack(shift(pack(*scan), "seq", 2 * reach)), scan)
        reach *= 2
    return combine(scan, before)[1]


def gather_columns(block):
    count = lax.axis_size("seq") // 2
    place = lax.axis_index("seq") // 2
    up, down = [block], [block]
    for step in range(1, count):
        up.append(shift(up[-1], "seq", 2))
        down.append(shift(down[-1], "seq", -2))
    slots = [block]
    for step in range(1, count):
        slots.append(jnp.where(place + step < count, down[step], up[count - step]))
    return [(slot, partner(slot, "seq", 0)) for slot in slots]


def project(normed, slots):
    count = len(slots)
    place, odd = lax.axis_index("seq") // 2, lax.axis_index("seq") % 2 == 1
    parts = []
    for pair in slots:
        first, second = (
            jnp.dot(normed, block, preferred_element_type=jnp.float32).astype(jnp.bfloat16)
            for block in pair
        )
        parts.append(
            jnp.concatenate(
                [jnp.where(odd, second, first), jnp.where(odd, first, second)], axis=1
            )
        )
    parts = jnp.stack(parts + parts[:-1])
    parts = lax.dynamic_slice_in_dim(parts, (count - place) % count, count, axis=0)
    return parts.transpose(1, 0, 2).reshape(normed.shape[0], -1)


def sum_rows(x, axis):
    size = lax.axis_size(axis)
    bits = size.bit_length() - 1
    width = x.shape[-1]
    x = x.reshape((2,) * bits + (-1, width))
    for bit in range(bits):
        mine = lax.axis_index(axis) >> bit & 1
        where = bits - 1 - bit
        keep = lax.dynamic_index_in_dim(x, mine, where, keepdims=False)
        give = lax.dynamic_index_in_dim(x, 1 - mine, where, keepdims=False)
        got = partner(give.astype(jnp.bfloat16), axis, bit)
        x = keep.astype(jnp.float32) + got.astype(jnp.float32)
    return x


def partner(x, axis, stride):
    return lax.ppermute(x, axis, [(i, i ^ 1 << stride) for i in range(lax.axis_size(axis))])


MESH = pl.DeviceIdType.MESH


def moe_kernel(
    planes, cols, cap, x_ref, info_ref, hidden_ref, up_hbm, down_hbm, out_ref,
    up, down, xz, iz, pk, rows, act, own, other, back, rb, pt, fin, total,
    weight_sem, sx, rx, si, ri, sp, rp, sf, rf, sb, rbk, sr, rr, sn, rn,
):
    seq, head = lax.axis_index("seq"), lax.axis_index("head")
    wide = cols // 2
    z, y, x, c = seq // 2, seq % 2, head // 2, head % 2
    k = y * wide + x
    count, width = x_ref.shape
    tile = width // 7 if width % (7 * 128) == 0 else width
    deep = width // 3 if width % (3 * 128) == 0 else width
    slots = cols * cap

    def in_plane(col):
        return {"seq": 2 * z + col // wide, "head": 2 * (col % wide) + c}

    def in_line(plane):
        return {"seq": 2 * plane + y, "head": head}

    mate = {"seq": seq, "head": 2 * x + 1 - c}

    def remote(src, dst, send, recv, device):
        return pltpu.make_async_remote_copy(
            src_ref=src, dst_ref=dst, send_sem=send, recv_sem=recv,
            device_id=device, device_id_type=MESH,
        )

    load_up = pltpu.make_async_copy(up_hbm.at[0], up, weight_sem.at[0])
    load_down = pltpu.make_async_copy(down_hbm.at[0], down, weight_sem.at[1])
    load_up.start()
    load_down.start()

    barrier = pltpu.get_barrier_semaphore()
    for d in range(1, planes):
        pl.semaphore_signal(
            barrier, inc=1, device_id=in_line((z + d) % planes), device_id_type=MESH
        )
    for j in range(1, cols):
        pl.semaphore_signal(
            barrier, inc=1, device_id=in_plane((k + j) % cols), device_id_type=MESH
        )
    pl.semaphore_signal(barrier, inc=1, device_id=mate, device_id_type=MESH)
    pl.semaphore_wait(barrier, planes + cols - 1)

    def line_rows(to):
        return remote(x_ref, xz.at[z], sx.at[to], rx.at[z], in_line(to))

    def line_info(to):
        return remote(info_ref.at[to], iz.at[z], si.at[to], ri.at[z], in_line(to))

    def spread(block, col):
        part = pl.ds(pl.multiple_of(col * cap, cap), cap)
        place = pl.ds(pl.multiple_of(k * cap, cap), cap)
        return remote(
            pk.at[block, part], rows.at[block, 0, place],
            sp.at[block, col], rp.at[block, k], in_plane(col),
        )

    def forward(block):
        return remote(rows.at[block, 0], rows.at[block, 1], sf.at[block], rf.at[block], mate)

    def half_back(block):
        return remote(other.at[block], back.at[block], sb.at[block], rbk.at[block], mate)

    def give_back(block, col):
        part = pl.ds(pl.multiple_of(col * cap, cap), cap)
        place = pl.ds(pl.multiple_of(k * cap, cap), cap)
        return remote(
            own.at[block, part], rb.at[block, place],
            sr.at[block, col], rr.at[block, k], in_plane(col),
        )

    def line_back(to):
        return remote(pt.at[to], fin.at[z], sn.at[to], rn.at[z], in_line(to))

    def got(dst, sem):
        pltpu.make_async_copy(dst, dst, sem).wait()

    for d in range(1, planes):
        line_rows((z + d) % planes).start()
        line_info((z + d) % planes).start()

    mine = pl.ds(pl.multiple_of(k * cap, cap), cap)

    def pack(d):
        block = (z + planes - d) % planes

        @pl.when(d == 0)
        def _():
            xz[z] = x_ref[...]
            iz[z] = info_ref[z]

        @pl.when(d > 0)
        def _():
            got(xz.at[block], rx.at[block])
            got(iz.at[block], ri.at[block])

        pk[block] = lax.dot_general(
            iz[block, pl.ds(0, count)], xz[block], (((0,), (0,)), ((), ())),
            preferred_element_type=jnp.float32,
        ).astype(jnp.bfloat16)
        for j in range(1, cols):
            spread(block, (k + j) % cols).start()
        rows[block, 0, mine] = pk[block, mine]

    def pass_on(d):
        block = (z + planes - d) % planes
        for j in range(1, cols):
            col = (k + j) % cols
            place = pl.ds(pl.multiple_of(col * cap, cap), cap)
            got(rows.at[block, 0, place], rp.at[block, col])
        forward(block).start()

    def compute(d):
        block = (z + planes - d) % planes

        @pl.when(d == 0)
        def _():
            load_up.wait()
            load_down.wait()

        got(rows.at[block, 1], rf.at[block])
        total[...] = jnp.zeros_like(total)

        def gather_up(i, carry):
            at = pl.ds(pl.multiple_of(i * deep, 128), deep)
            taken = rows[block, :, :, at].reshape(2 * slots, deep)
            total[...] += jnp.dot(taken, up[at, :], preferred_element_type=jnp.float32)
            return carry

        lax.fori_loop(0, width // deep, gather_up, 0)
        kept = jnp.maximum(total[...], 0.0)
        act[...] = (kept * kept).astype(jnp.bfloat16)

        def gather_down(i, carry):
            at = pl.ds(pl.multiple_of(i * tile, 128), tile)
            result = jnp.dot(act[...], down[:, at], preferred_element_type=jnp.float32)
            result = result.astype(jnp.bfloat16)
            own[block, :, at] = result[:slots]
            other[block, :, at] = result[slots:]
            return carry

        lax.fori_loop(0, width // tile, gather_down, 0)
        half_back(block).start()

    def add_halves(d):
        block = (z + planes - d) % planes
        got(back.at[block], rbk.at[block])
        own[block] = (
            own[block].astype(jnp.float32) + back[block].astype(jnp.float32)
        ).astype(jnp.bfloat16)
        for j in range(1, cols):
            give_back(block, (k + j) % cols).start()
        rb[block, mine] = own[block, mine]

    def combine(d):
        block = (z + planes - d) % planes
        for j in range(1, cols):
            col = (k + j) % cols
            place = pl.ds(pl.multiple_of(col * cap, cap), cap)
            got(rb.at[block, place], rr.at[block, col])
        pt[block] = jnp.dot(
            iz[block, pl.ds(count, count)], rb[block], preferred_element_type=jnp.float32
        ).astype(jnp.bfloat16)

        @pl.when(d > 0)
        def _():
            line_back(block).start()

    def step(t, carry):
        for lag, stage in ((0, pack), (2, compute), (1, pass_on), (3, add_halves), (4, combine)):

            @pl.when((t >= lag) & (t < planes + lag))
            def _(lag=lag, stage=stage):
                stage(t - lag)

        return carry

    lax.fori_loop(0, planes + 4, step, 0)

    answer = hidden_ref[...] + pt[z].astype(jnp.float32)
    for d in range(1, planes):
        block = (z + planes - d) % planes
        got(fin.at[block], rn.at[block])
        answer += fin[block].astype(jnp.float32)
    out_ref[...] = answer.astype(out_ref.dtype)

    for d in range(1, planes):
        to = (z + d) % planes
        line_rows(to).wait_send()
        line_info(to).wait_send()
        line_back(to).wait_send()

    def finish(block, carry):
        for j in range(1, cols):
            spread(block, (k + j) % cols).wait_send()
            give_back(block, (k + j) % cols).wait_send()
        forward(block).wait_send()
        half_back(block).wait_send()
        return carry

    lax.fori_loop(0, planes, finish, 0)


def expert_layer(inputs, info, hidden, up_weight, down_weight, planes, cols, cap):
    count, width = inputs.shape
    units = up_weight.shape[2]
    slots = cols * cap
    dma = pltpu.SemaphoreType.DMA
    bf16 = jnp.bfloat16
    vmem = pl.BlockSpec(memory_space=pltpu.VMEM)
    return pl.pallas_call(
        functools.partial(moe_kernel, planes, cols, cap),
        out_shape=jax.ShapeDtypeStruct((count, width), bf16),
        in_specs=[vmem, vmem, vmem, pl.BlockSpec(memory_space=pl.ANY), pl.BlockSpec(memory_space=pl.ANY)],
        out_specs=vmem,
        scratch_shapes=[
            pltpu.VMEM((width, units), bf16),
            pltpu.VMEM((units, width), bf16),
            pltpu.VMEM((planes, count, width), bf16),
            pltpu.VMEM((planes, 2 * count, slots), bf16),
            pltpu.VMEM((planes, slots, width), bf16),
            pltpu.VMEM((planes, 2, slots, width), bf16),
            pltpu.VMEM((2 * slots, units), bf16),
            pltpu.VMEM((planes, slots, width), bf16),
            pltpu.VMEM((planes, slots, width), bf16),
            pltpu.VMEM((planes, slots, width), bf16),
            pltpu.VMEM((planes, slots, width), bf16),
            pltpu.VMEM((planes, count, width), bf16),
            pltpu.VMEM((planes, count, width), bf16),
            pltpu.VMEM((2 * slots, units), jnp.float32),
            dma((2,)),
            dma((planes,)), dma((planes,)), dma((planes,)), dma((planes,)),
            dma((planes, cols)), dma((planes, cols)),
            dma((planes,)), dma((planes,)), dma((planes,)), dma((planes,)),
            dma((planes, cols)), dma((planes, cols)),
            dma((planes,)), dma((planes,)),
        ],
        compiler_params=pltpu.CompilerParams(
            collective_id=1, has_side_effects=True, vmem_limit_bytes=60 * 1024 * 1024
        ),
        cost_estimate=pl.CostEstimate(
            flops=8 * planes * slots * width * units,
            bytes_accessed=4 * width * units,
            transcendentals=0,
        ),
    )(inputs, info, hidden, up_weight, down_weight)


def per_device(
    ssm_values,
    ssm_gate,
    write_proj,
    read_proj,
    step_size,
    decay_power,
    skip_gain,
    norm_gain,
    out_weight,
    residual,
    expert_norm,
    router_weight,
    expert_index,
    up_weight,
    down_weight,
):
    slots = gather_columns(out_weight)
    tokens_dev = ssm_values.shape[0]
    heads_dev = step_size.shape[1]
    per_group = HEADS // GROUPS
    groups_dev = heads_dev // per_group
    count_blocks = tokens_dev // BLOCK_LEN
    decay_rates = jnp.exp2(-decay_power.astype(jnp.float32))
    values = ssm_values.reshape(count_blocks, BLOCK_LEN, heads_dev, HEAD_DIM)
    steps_all = step_size.reshape(count_blocks, BLOCK_LEN, heads_dev)
    writes = write_proj.reshape(count_blocks, BLOCK_LEN, groups_dev, STATE)
    reads = read_proj.reshape(count_blocks, BLOCK_LEN, groups_dev, STATE)
    causal = jnp.tril(jnp.ones((BLOCK_LEN, BLOCK_LEN), dtype=bool))

    def one_block(pieces):
        values_in, steps_in, write_in, read_in = pieces
        log_decay = -steps_in * decay_rates[None, :]
        cumulative = jnp.cumsum(log_decay, axis=0)
        scores = jnp.einsum("tgn,sgn->gts", read_in, write_in, preferred_element_type=jnp.float32)
        scores = jnp.repeat(scores, per_group, axis=0)
        decays = jnp.exp(cumulative.T[:, :, None] - cumulative.T[:, None, :])
        mixing = jnp.where(causal[None], scores * decays * steps_in.T[:, None, :], 0.0).astype(
            jnp.bfloat16
        )
        inner_out = jnp.einsum(
            "hts,shp->thp", mixing, values_in, preferred_element_type=jnp.float32
        )
        block_total = cumulative[-1]
        weighted = (
            values_in.astype(jnp.float32)
            * (jnp.exp(block_total[None, :] - cumulative) * steps_in)[:, :, None]
        ).astype(jnp.bfloat16)
        write_heads = jnp.repeat(write_in, per_group, axis=1)
        fresh_state = jnp.einsum(
            "shp,shn->hpn", weighted, write_heads, preferred_element_type=jnp.float32
        )
        return (inner_out, fresh_state, block_total, cumulative)

    inner_all, fresh_all, totals_blk, cumul_all = lax.map(
        one_block, (values, steps_all, writes, reads)
    )

    def summarize(carried_in, pieces):
        decay_prod, summary = carried_in
        block_total, fresh_state = pieces
        factor = jnp.exp(block_total)
        return ((decay_prod * factor, factor[:, None, None] * summary + fresh_state), None)

    zero_state = jnp.zeros((heads_dev, HEAD_DIM, STATE), jnp.float32)
    (device_decay, device_state), unused = lax.scan(
        summarize, (jnp.ones((heads_dev,), jnp.float32), zero_state), (totals_blk, fresh_all)
    )

    incoming = entering(device_decay, device_state)

    def emit_rows(carry_state, pieces):
        read_in, cumulative, block_total, fresh_state = pieces
        read_heads = jnp.repeat(read_in, per_group, axis=1)
        carried = jnp.einsum(
            "thn,hpn->thp",
            read_heads,
            carry_state.astype(jnp.bfloat16),
            preferred_element_type=jnp.float32,
        )
        carried = carried * jnp.exp(cumulative)[:, :, None]
        return (jnp.exp(block_total)[:, None, None] * carry_state + fresh_state, carried)

    final_state, carried_all = lax.scan(
        emit_rows, incoming, (reads, cumul_all, totals_blk, fresh_all)
    )
    values_flat = ssm_values.reshape(tokens_dev, heads_dev, HEAD_DIM).astype(jnp.float32)
    ssm_out = (inner_all + carried_all).reshape(tokens_dev, heads_dev, HEAD_DIM) + skip_gain[
        None, :, None
    ] * values_flat
    gate_vals = ssm_gate.reshape(tokens_dev, heads_dev, HEAD_DIM).astype(jnp.float32)
    gated = (ssm_out * jax.nn.silu(gate_vals)).reshape(tokens_dev, groups_dev, per_group * HEAD_DIM)
    inv_rms = lax.rsqrt(jnp.mean(gated * gated, axis=-1, keepdims=True) + EPSILON)
    normed = (
        (gated * inv_rms).reshape(tokens_dev, heads_dev * HEAD_DIM) * norm_gain[None, :]
    ).astype(jnp.bfloat16)
    rows_own = tokens_dev // lax.axis_size("head")
    mixed_out = sum_rows(project(normed, slots), "head")
    hidden = residual.astype(jnp.float32) + mixed_out
    inputs = (
        hidden
        * lax.rsqrt(jnp.mean(hidden * hidden, axis=-1, keepdims=True) + EPSILON)
        * expert_norm[None, :]
    ).astype(jnp.bfloat16)
    logits = jnp.dot(inputs, router_weight, preferred_element_type=jnp.float32)
    experts = router_weight.shape[1]
    model_width = inputs.shape[1]
    expert_hits = expert_index[:, :, None] == jnp.arange(experts, dtype=jnp.int32)[None, None, :]
    picked = jnp.sum(jnp.where(expert_hits, logits[:, None, :], 0.0), axis=-1)
    probability = jax.nn.sigmoid(picked)
    shares = ROUTE_SCALE * probability / jnp.sum(probability, axis=1, keepdims=True)
    capacity = (
        8
        * TOP
        * tokens_dev
        // (3 * lax.axis_size("seq") * lax.axis_size("head") * lax.axis_size("head"))
    )
    flat_hits = expert_hits.astype(jnp.int32).reshape(rows_own * TOP, experts)
    before = jnp.cumsum(flat_hits, axis=0) - flat_hits
    slot_index = jnp.sum(before * flat_hits, axis=1)
    cols = lax.axis_size("head")
    planes = lax.axis_size("seq") // 2
    cap = -(-capacity // 16) * 16
    target = expert_index * cap + slot_index.reshape(rows_own, TOP)
    chosen = target[:, :, None] == jnp.arange(experts * cap, dtype=jnp.int32)[None, None, :]
    place = jnp.any(chosen, axis=1).astype(jnp.bfloat16)
    weigh = jnp.sum(jnp.where(chosen, shares[:, :, None], 0.0), axis=1).astype(jnp.bfloat16)
    info = jnp.concatenate([place, weigh], axis=0)
    info = info.reshape(2 * rows_own, planes, cols * cap).transpose(1, 0, 2)
    return expert_layer(inputs, info, hidden, up_weight, down_weight, planes, cols, cap)


def solution(mesh):
    return jax.shard_map(
        per_device,
        mesh=mesh,
        in_specs=(
            P(("grp", "seq"), "head"),
            P(("grp", "seq"), "head"),
            P(("grp", "seq"), "head"),
            P(("grp", "seq"), "head"),
            P(("grp", "seq"), "head"),
            P("head"),
            P("head"),
            P("head"),
            P("head", "seq"),
            P(("grp", "seq", "head"), None),
            P(),
            P(),
            P(("grp", "seq", "head"), None),
            P(("seq", "head"), None, None),
            P(("seq", "head"), None, None),
        ),
        out_specs=P(("grp", "seq", "head"), None),
        check_vma=False,
    )
```

```python
import functools
import jax
import jax.numpy as jnp
from jax import lax
from jax.experimental import pallas as pl
from jax.experimental.pallas import tpu as pltpu
from jax.sharding import PartitionSpec as P

HEADS = 64
HEAD_DIM = 64
STATE = 128
TOP = 6


EPSILON = 1e-05
ROUTE_SCALE = 2.5
MESH = pl.DeviceIdType.MESH


def mixer_kernel(
    pairs, heads_mesh, value_ref, gate_ref, write_ref, read_ref, cum_ref, cum_t_ref, step_t_ref,
    coef_ref, ecum_ref, decay_ref, skip_ref, gain_ref, weight_ref, out_ref,
    blocks, fresh, y_send, y_got, z_send, z_got, carry, mixed, normed, prod, sums,
    su, sd, sy, rw, s_state, r_state, ss, rs,
):
    seq, head = lax.axis_index("seq"), lax.axis_index("head")
    z, y = seq // 2, seq % 2
    mate = {"seq": 2 * z + 1 - y}
    above, below = {"seq": seq + 2}, {"seq": seq - 2}
    count = value_ref.shape[0]
    heads = cum_ref.shape[1]
    groups = write_ref.shape[1] // STATE
    per_group = heads // groups
    lanes = per_group * HEAD_DIM
    columns = weight_ref.shape[0]
    pieces = 3 if columns % 48 == 0 else 1
    piece = columns // pieces
    own_rows = count // heads_mesh
    flat = heads * HEAD_DIM

    def remote(src, dst, send, recv, device):
        return pltpu.make_async_remote_copy(
            src_ref=src, dst_ref=dst, send_sem=send, recv_sem=recv,
            device_id=device, device_id_type=MESH,
        )

    def got(dst, sem):
        pltpu.make_async_copy(dst, dst, sem).wait()

    barrier = pltpu.get_barrier_semaphore()

    def greet(device):
        pl.semaphore_signal(barrier, inc=1, device_id=device, device_id_type=MESH)

    greet(mate)
    for j in range(1, heads_mesh):
        greet({"head": (head + j) % heads_mesh})

    @pl.when(z < pairs - 1)
    def _():
        greet(above)

    @pl.when(z > 0)
    def _():
        greet(below)

    blocks[seq] = weight_ref[...]
    ends = jnp.where(z < pairs - 1, 1, 0) + jnp.where(z > 0, 1, 0)
    pl.semaphore_wait(barrier, heads_mesh + ends)

    def piece_of(source, i):
        return blocks.at[source, pl.ds(i * piece, piece)]

    def weight_copy(source, i, sems, device):
        here = piece_of(source, i)
        return remote(here, here, sems.at[source, i], rw.at[source, i], device)

    @pl.when(z < pairs - 1)
    def _():
        for i in range(pieces):
            weight_copy(seq, i, su, above).start()

    @pl.when(z > 0)
    def _():
        for i in range(pieces):
            weight_copy(seq, i, sd, below).start()

    low = lax.broadcasted_iota(jnp.int32, (count, 2 * HEAD_DIM), 1) < HEAD_DIM

    def two_heads(ref, h):
        return jnp.where(low, ref[:, h : h + 1], ref[:, h + 1 : h + 2])

    for h in range(0, heads, 2):
        g = h // per_group
        at = slice(h * HEAD_DIM, (h + 2) * HEAD_DIM)
        weighted = (value_ref[:, at].astype(jnp.float32) * two_heads(coef_ref, h)).astype(
            jnp.bfloat16
        )
        fresh[at, :] = lax.dot_general(
            weighted, write_ref[:, g * STATE : (g + 1) * STATE], (((0,), (0,)), ((), ())),
            preferred_element_type=jnp.float32,
        )
    y_send[:flat] = fresh[...].astype(jnp.bfloat16)
    y_send[flat:] = decay_ref[...].astype(jnp.bfloat16)
    state_y = remote(y_send, y_got, s_state.at[0], r_state.at[0], mate)
    state_y.start()
    for i in range(pieces):
        weight_copy(seq, i, sy, mate).start()

    causal = lax.broadcasted_iota(jnp.int32, (count, count), 0) >= lax.broadcasted_iota(
        jnp.int32, (count, count), 1
    )

    def inner(g):
        where = slice(g * STATE, (g + 1) * STATE)
        scores = lax.dot_general(
            read_ref[:, where], write_ref[:, where], (((1,), (1,)), ((), ())),
            preferred_element_type=jnp.float32,
        )
        for h in range(g * per_group, (g + 1) * per_group, 2):
            at = slice(h * HEAD_DIM, (h + 2) * HEAD_DIM)
            sides = []
            for n in (h, h + 1):
                decays = jnp.exp(
                    jnp.where(causal, cum_ref[:, n : n + 1] - cum_t_ref[n : n + 1, :], 0.0)
                )
                mixing = jnp.where(causal, scores * decays * step_t_ref[n : n + 1, :], 0.0)
                sides.append(
                    jnp.dot(
                        mixing.astype(jnp.bfloat16), value_ref[:, at],
                        preferred_element_type=jnp.float32,
                    )
                )
            mixed[:, at] = jnp.where(low, sides[0], sides[1]) + skip_ref[
                :, at
            ] * value_ref[:, at].astype(jnp.float32)

    def spread(decay):
        wide = jnp.broadcast_to(decay[:heads, None, :], (heads, HEAD_DIM, STATE))
        return wide.reshape(flat, STATE)

    def relay(k):
        for valid, onward, source, sems, device in (
            (z >= k, z < pairs - 1, seq - 2 * k, su, above),
            (z + k < pairs, z > 0, seq + 2 * k, sd, below),
        ):

            @pl.when(valid)
            def _(onward=onward, source=source, sems=sems, device=device):
                for i in range(pieces):
                    got(piece_of(source, i), rw.at[source, i])

                    @pl.when(onward)
                    def _():
                        weight_copy(source, i, sems, device).start()

                    weight_copy(source, i, sy, mate).start()

    inner(0)
    state_y.wait()
    theirs = y_got[:flat].astype(jnp.float32)
    their_decay = spread(y_got[flat:].astype(jnp.float32))
    my_decay = spread(decay_ref[...])
    pair_state = jnp.where(
        y == 1, my_decay * theirs + fresh[...], their_decay * fresh[...] + theirs
    )
    state_z = remote(z_send, z_got, s_state.at[1], r_state.at[1], above)

    @pl.when(z == 0)
    def _():
        z_send[...] = pair_state.astype(jnp.bfloat16)
        z_got[...] = jnp.zeros_like(z_got)
        state_z.start()

    for g in range(1, groups):
        inner(g)
    relay(1)

    @pl.when(z > 0)
    def _():
        got(z_got, r_state.at[1])

        @pl.when(z < pairs - 1)
        def _():
            z_send[...] = (
                my_decay * their_decay * z_got[...].astype(jnp.float32) + pair_state
            ).astype(jnp.bfloat16)
            state_z.start()

    entered = z_got[...].astype(jnp.float32)
    carry[...] = jnp.where(y == 1, their_decay * entered + theirs, entered).astype(jnp.bfloat16)
    for g in range(groups):
        at = slice(g * lanes, (g + 1) * lanes)
        carried = lax.dot_general(
            read_ref[:, g * STATE : (g + 1) * STATE], carry[at, :], (((1,), (1,)), ((), ())),
            preferred_element_type=jnp.float32,
        )
        scale = jnp.concatenate(
            [two_heads(ecum_ref, h) for h in range(g * per_group, (g + 1) * per_group, 2)], axis=1
        )
        gate = gate_ref[:, at].astype(jnp.float32)
        gated = (mixed[:, at] + carried * scale) * (gate * jax.nn.sigmoid(gate))
        inv_rms = lax.rsqrt(jnp.mean(gated * gated, axis=-1, keepdims=True) + EPSILON)
        normed[:, at] = (gated * inv_rms * gain_ref[:, at]).astype(jnp.bfloat16)

    def chunk_of(source, to):
        rows = pl.ds(pl.multiple_of(to * own_rows, own_rows), own_rows)
        return prod.at[source, rows]

    def give(source, to):
        return remote(
            chunk_of(source, to), sums.at[source, head], ss.at[source, to], rs.at[source, head],
            {"head": to},
        )

    def project(source):
        prod[source, :, pl.ds(0, columns)] = lax.dot_general(
            normed[...], blocks[source], (((1,), (1,)), ((), ())),
            preferred_element_type=jnp.float32,
        ).astype(jnp.bfloat16)
        for j in range(1, heads_mesh):
            give(source, (head + j) % heads_mesh).start()

    def arrived(source):
        for i in range(pieces):
            got(piece_of(source, i), rw.at[source, i])

    across = 1 - 2 * y
    prod[...] = jnp.zeros_like(prod)
    project(seq)
    for k in range(1, pairs):
        if k > 1:
            relay(k)
        if k == 1:
            arrived(seq + across)
            project(seq + across)
        for valid, source in ((z >= k, seq - 2 * k), (z + k < pairs, seq + 2 * k)):

            @pl.when(valid)
            def _(source=source):
                project(source)

        for valid, source in ((z >= k, seq - 2 * k), (z + k < pairs, seq + 2 * k)):

            @pl.when(valid)
            def _(source=source):
                arrived(source + across)
                project(source + across)

    def collect(source, carry_on):
        rows = pl.ds(pl.multiple_of(head * own_rows, own_rows), own_rows)
        total = prod[source, rows].astype(jnp.float32)
        for j in range(1, heads_mesh):
            other = (head + j) % heads_mesh
            got(sums.at[source, other], rs.at[source, other])
            total += sums[source, other].astype(jnp.float32)
        out_ref[source] = total
        return carry_on

    lax.fori_loop(0, 2 * pairs, collect, 0)

    @pl.when(z < pairs - 1)
    def _():
        state_z.wait_send()
        for i in range(pieces):
            weight_copy(seq, i, su, above).wait_send()

    @pl.when(z > 0)
    def _():
        for i in range(pieces):
            weight_copy(seq, i, sd, below).wait_send()

    for k in range(pairs):
        for valid, onward, source, sems, device in (
            (z >= k, z < pairs - 1, seq - 2 * k, su, above),
            (z + k < pairs, z > 0, seq + 2 * k, sd, below),
        ):
            if k == 0 and sems is sd:
                continue

            @pl.when(valid)
            def _(k=k, onward=onward, source=source, sems=sems, device=device):
                for i in range(pieces):
                    weight_copy(source, i, sy, mate).wait_send()
                    if k > 0:

                        @pl.when(onward)
                        def _():
                            weight_copy(source, i, sems, device).wait_send()

    def sent(source, carry_on):
        for j in range(1, heads_mesh):
            give(source, (head + j) % heads_mesh).wait_send()
        return carry_on

    lax.fori_loop(0, 2 * pairs, sent, 0)


def mixer(values, gates, writes, reads, cumulative, steps, skip_gain, norm_gain, weight):
    count, heads = cumulative.shape
    pairs, heads_mesh = lax.axis_size("seq") // 2, lax.axis_size("head")
    total = cumulative[-1:]
    coef = jnp.exp(total - cumulative) * steps
    decay = jnp.zeros((16, STATE), jnp.float32).at[:heads].set(
        jnp.broadcast_to(jnp.exp(total).T, (heads, STATE))
    )
    turned = weight.T
    columns, rows = turned.shape
    flat = heads * HEAD_DIM
    padded = -(-columns // 128) * 128
    pieces = 3 if columns % 48 == 0 else 1
    size = 2 * pairs
    dma = pltpu.SemaphoreType.DMA
    bf16 = jnp.bfloat16
    vmem = pl.BlockSpec(memory_space=pltpu.VMEM)
    out = pl.pallas_call(
        functools.partial(mixer_kernel, pairs, heads_mesh),
        out_shape=jax.ShapeDtypeStruct((size, count // heads_mesh, padded), jnp.float32),
        in_specs=[vmem] * 13,
        out_specs=vmem,
        scratch_shapes=[
            pltpu.VMEM((size, columns, rows), bf16),
            pltpu.VMEM((flat, STATE), jnp.float32),
            pltpu.VMEM((flat + 16, STATE), bf16),
            pltpu.VMEM((flat + 16, STATE), bf16),
            pltpu.VMEM((flat, STATE), bf16),
            pltpu.VMEM((flat, STATE), bf16),
            pltpu.VMEM((flat, STATE), bf16),
            pltpu.VMEM((count, flat), jnp.float32),
            pltpu.VMEM((count, flat), bf16),
            pltpu.VMEM((size, count, padded), bf16),
            pltpu.VMEM((size, heads_mesh, count // heads_mesh, padded), bf16),
            dma((size, pieces)), dma((size, pieces)), dma((size, pieces)), dma((size, pieces)),
            dma((2,)), dma((2,)),
            dma((size, heads_mesh)), dma((size, heads_mesh)),
        ],
        compiler_params=pltpu.CompilerParams(
            collective_id=0, has_side_effects=True, vmem_limit_bytes=48 * 1024 * 1024
        ),
    )(
        values, gates, writes, reads, cumulative, cumulative.T, steps.T, coef,
        jnp.exp(cumulative), decay, jnp.repeat(skip_gain, HEAD_DIM)[None], norm_gain[None], turned,
    )
    return out[:, :, :columns].transpose(1, 0, 2).reshape(count // heads_mesh, size * columns)


def moe_kernel(
    planes, cols, cap, x_ref, info_ref, hidden_ref, up_hbm, down_hbm, out_ref,
    up, down, xz, iz, pk, rows, act, own, other, back, rb, pt, fin, total,
    weight_sem, sx, rx, si, ri, sp, rp, sf, rf, sb, rbk, sr, rr, sn, rn,
):
    seq, head = lax.axis_index("seq"), lax.axis_index("head")
    wide = cols // 2
    z, y, x, c = seq // 2, seq % 2, head // 2, head % 2
    k = y * wide + x
    count, width = x_ref.shape
    tile = width // 7 if width % (7 * 128) == 0 else width
    deep = width // 3 if width % (3 * 128) == 0 else width
    slots = cols * cap

    def in_plane(col):
        return {"seq": 2 * z + col // wide, "head": 2 * (col % wide) + c}

    def in_line(plane):
        return {"seq": 2 * plane + y, "head": head}

    mate = {"seq": seq, "head": 2 * x + 1 - c}

    def remote(src, dst, send, recv, device):
        return pltpu.make_async_remote_copy(
            src_ref=src, dst_ref=dst, send_sem=send, recv_sem=recv,
            device_id=device, device_id_type=MESH,
        )

    load_up = pltpu.make_async_copy(up_hbm.at[0], up, weight_sem.at[0])
    load_down = pltpu.make_async_copy(down_hbm.at[0], down, weight_sem.at[1])
    load_up.start()
    load_down.start()

    barrier = pltpu.get_barrier_semaphore()
    for d in range(1, planes):
        pl.semaphore_signal(
            barrier, inc=1, device_id=in_line((z + d) % planes), device_id_type=MESH
        )
    for j in range(1, cols):
        pl.semaphore_signal(
            barrier, inc=1, device_id=in_plane((k + j) % cols), device_id_type=MESH
        )
    pl.semaphore_signal(barrier, inc=1, device_id=mate, device_id_type=MESH)
    pl.semaphore_wait(barrier, planes + cols - 1)

    def line_rows(to):
        return remote(x_ref, xz.at[z], sx.at[to], rx.at[z], in_line(to))

    def line_info(to):
        return remote(info_ref.at[to], iz.at[z], si.at[to], ri.at[z], in_line(to))

    def spread(block, col):
        part = pl.ds(pl.multiple_of(col * cap, cap), cap)
        place = pl.ds(pl.multiple_of(k * cap, cap), cap)
        return remote(
            pk.at[block, part], rows.at[block, 0, place],
            sp.at[block, col], rp.at[block, k], in_plane(col),
        )

    def forward(block):
        return remote(rows.at[block, 0], rows.at[block, 1], sf.at[block], rf.at[block], mate)

    def half_back(block):
        return remote(other.at[block], back.at[block], sb.at[block], rbk.at[block], mate)

    def give_back(block, col):
        part = pl.ds(pl.multiple_of(col * cap, cap), cap)
        place = pl.ds(pl.multiple_of(k * cap, cap), cap)
        return remote(
            own.at[block, part], rb.at[block, place],
            sr.at[block, col], rr.at[block, k], in_plane(col),
        )

    def line_back(to):
        return remote(pt.at[to], fin.at[z], sn.at[to], rn.at[z], in_line(to))

    def got(dst, sem):
        pltpu.make_async_copy(dst, dst, sem).wait()

    for d in range(1, planes):
        line_rows((z + d) % planes).start()
        line_info((z + d) % planes).start()

    mine = pl.ds(pl.multiple_of(k * cap, cap), cap)

    def pack(d):
        block = (z + planes - d) % planes

        @pl.when(d == 0)
        def _():
            xz[z] = x_ref[...]
            iz[z] = info_ref[z]

        @pl.when(d > 0)
        def _():
            got(xz.at[block], rx.at[block])
            got(iz.at[block], ri.at[block])

        pk[block] = lax.dot_general(
            iz[block, pl.ds(0, count)], xz[block], (((0,), (0,)), ((), ())),
            preferred_element_type=jnp.float32,
        ).astype(jnp.bfloat16)
        for j in range(1, cols):
            spread(block, (k + j) % cols).start()
        rows[block, 0, mine] = pk[block, mine]

    def pass_on(d):
        block = (z + planes - d) % planes
        for j in range(1, cols):
            col = (k + j) % cols
            place = pl.ds(pl.multiple_of(col * cap, cap), cap)
            got(rows.at[block, 0, place], rp.at[block, col])
        forward(block).start()

    def compute(d):
        block = (z + planes - d) % planes

        @pl.when(d == 0)
        def _():
            load_up.wait()
            load_down.wait()

        got(rows.at[block, 1], rf.at[block])
        total[...] = jnp.zeros_like(total)

        def gather_up(i, carry):
            at = pl.ds(pl.multiple_of(i * deep, 128), deep)
            taken = rows[block, :, :, at].reshape(2 * slots, deep)
            total[...] += lax.dot_general(
                taken, up[:, at], (((1,), (1,)), ((), ())), preferred_element_type=jnp.float32
            )
            return carry

        lax.fori_loop(0, width // deep, gather_up, 0)
        kept = jnp.maximum(total[...], 0.0)
        act[...] = (kept * kept).astype(jnp.bfloat16)

        def gather_down(i, carry):
            at = pl.ds(pl.multiple_of(i * tile, 128), tile)
            result = jnp.dot(act[...], down[:, at], preferred_element_type=jnp.float32)
            result = result.astype(jnp.bfloat16)
            own[block, :, at] = result[:slots]
            other[block, :, at] = result[slots:]
            return carry

        lax.fori_loop(0, width // tile, gather_down, 0)
        half_back(block).start()

    def add_halves(d):
        block = (z + planes - d) % planes
        got(back.at[block], rbk.at[block])
        own[block] = (
            own[block].astype(jnp.float32) + back[block].astype(jnp.float32)
        ).astype(jnp.bfloat16)
        for j in range(1, cols):
            give_back(block, (k + j) % cols).start()
        rb[block, mine] = own[block, mine]

    def combine(d):
        block = (z + planes - d) % planes
        for j in range(1, cols):
            col = (k + j) % cols
            place = pl.ds(pl.multiple_of(col * cap, cap), cap)
            got(rb.at[block, place], rr.at[block, col])
        pt[block] = jnp.dot(
            iz[block, pl.ds(count, count)], rb[block], preferred_element_type=jnp.float32
        ).astype(jnp.bfloat16)

        @pl.when(d > 0)
        def _():
            line_back(block).start()

    def step(t, carry):
        for lag, stage in ((0, pack), (2, compute), (1, pass_on), (3, add_halves), (4, combine)):

            @pl.when((t >= lag) & (t < planes + lag))
            def _(lag=lag, stage=stage):
                stage(t - lag)

        return carry

    lax.fori_loop(0, planes + 4, step, 0)

    answer = hidden_ref[...] + pt[z].astype(jnp.float32)
    for d in range(1, planes):
        block = (z + planes - d) % planes
        got(fin.at[block], rn.at[block])
        answer += fin[block].astype(jnp.float32)
    out_ref[...] = answer.astype(out_ref.dtype)

    for d in range(1, planes):
        to = (z + d) % planes
        line_rows(to).wait_send()
        line_info(to).wait_send()
        line_back(to).wait_send()

    def finish(block, carry):
        for j in range(1, cols):
            spread(block, (k + j) % cols).wait_send()
            give_back(block, (k + j) % cols).wait_send()
        forward(block).wait_send()
        half_back(block).wait_send()
        return carry

    lax.fori_loop(0, planes, finish, 0)


def expert_layer(inputs, info, hidden, up_weight, down_weight, planes, cols, cap):
    count, width = inputs.shape
    units = up_weight.shape[2]
    slots = cols * cap
    dma = pltpu.SemaphoreType.DMA
    bf16 = jnp.bfloat16
    vmem = pl.BlockSpec(memory_space=pltpu.VMEM)
    return pl.pallas_call(
        functools.partial(moe_kernel, planes, cols, cap),
        out_shape=jax.ShapeDtypeStruct((count, width), bf16),
        in_specs=[vmem, vmem, vmem, pl.BlockSpec(memory_space=pl.ANY), pl.BlockSpec(memory_space=pl.ANY)],
        out_specs=vmem,
        scratch_shapes=[
            pltpu.VMEM((units, width), bf16),
            pltpu.VMEM((units, width), bf16),
            pltpu.VMEM((planes, count, width), bf16),
            pltpu.VMEM((planes, 2 * count, slots), bf16),
            pltpu.VMEM((planes, slots, width), bf16),
            pltpu.VMEM((planes, 2, slots, width), bf16),
            pltpu.VMEM((2 * slots, units), bf16),
            pltpu.VMEM((planes, slots, width), bf16),
            pltpu.VMEM((planes, slots, width), bf16),
            pltpu.VMEM((planes, slots, width), bf16),
            pltpu.VMEM((planes, slots, width), bf16),
            pltpu.VMEM((planes, count, width), bf16),
            pltpu.VMEM((planes, count, width), bf16),
            pltpu.VMEM((2 * slots, units), jnp.float32),
            dma((2,)),
            dma((planes,)), dma((planes,)), dma((planes,)), dma((planes,)),
            dma((planes, cols)), dma((planes, cols)),
            dma((planes,)), dma((planes,)), dma((planes,)), dma((planes,)),
            dma((planes, cols)), dma((planes, cols)),
            dma((planes,)), dma((planes,)),
        ],
        compiler_params=pltpu.CompilerParams(
            collective_id=1, has_side_effects=True, vmem_limit_bytes=60 * 1024 * 1024
        ),
        cost_estimate=pl.CostEstimate(
            flops=8 * planes * slots * width * units,
            bytes_accessed=4 * width * units,
            transcendentals=0,
        ),
    )(inputs, info, hidden, up_weight.swapaxes(1, 2), down_weight)


def per_device(
    ssm_values,
    ssm_gate,
    write_proj,
    read_proj,
    step_size,
    decay_power,
    skip_gain,
    norm_gain,
    out_weight,
    residual,
    expert_norm,
    router_weight,
    expert_index,
    up_weight,
    down_weight,
):
    tokens_dev = ssm_values.shape[0]
    decay_rates = jnp.exp2(-decay_power.astype(jnp.float32))
    cumulative = jnp.cumsum(-step_size * decay_rates[None, :], axis=0)
    mixed_out = mixer(
        ssm_values, ssm_gate, write_proj, read_proj, cumulative, step_size, skip_gain, norm_gain,
        out_weight,
    )
    rows_own = tokens_dev // lax.axis_size("head")
    hidden = residual.astype(jnp.float32) + mixed_out
    inputs = (
        hidden
        * lax.rsqrt(jnp.mean(hidden * hidden, axis=-1, keepdims=True) + EPSILON)
        * expert_norm[None, :]
    ).astype(jnp.bfloat16)
    logits = jnp.dot(inputs, router_weight, preferred_element_type=jnp.float32)
    experts = router_weight.shape[1]
    model_width = inputs.shape[1]
    expert_hits = expert_index[:, :, None] == jnp.arange(experts, dtype=jnp.int32)[None, None, :]
    picked = jnp.sum(jnp.where(expert_hits, logits[:, None, :], 0.0), axis=-1)
    probability = jax.nn.sigmoid(picked)
    shares = ROUTE_SCALE * probability / jnp.sum(probability, axis=1, keepdims=True)
    capacity = (
        8
        * TOP
        * tokens_dev
        // (3 * lax.axis_size("seq") * lax.axis_size("head") * lax.axis_size("head"))
    )
    flat_hits = expert_hits.astype(jnp.int32).reshape(rows_own * TOP, experts)
    before = jnp.cumsum(flat_hits, axis=0) - flat_hits
    slot_index = jnp.sum(before * flat_hits, axis=1)
    cols = lax.axis_size("head")
    planes = lax.axis_size("seq") // 2
    cap = -(-capacity // 16) * 16
    target = expert_index * cap + slot_index.reshape(rows_own, TOP)
    chosen = target[:, :, None] == jnp.arange(experts * cap, dtype=jnp.int32)[None, None, :]
    place = jnp.any(chosen, axis=1).astype(jnp.bfloat16)
    weigh = jnp.sum(jnp.where(chosen, shares[:, :, None], 0.0), axis=1).astype(jnp.bfloat16)
    info = jnp.concatenate([place, weigh], axis=0)
    info = info.reshape(2 * rows_own, planes, cols * cap).transpose(1, 0, 2)
    return expert_layer(inputs, info, hidden, up_weight, down_weight, planes, cols, cap)


def solution(mesh):
    return jax.shard_map(
        per_device,
        mesh=mesh,
        in_specs=(
            P(("grp", "seq"), "head"),
            P(("grp", "seq"), "head"),
            P(("grp", "seq"), "head"),
            P(("grp", "seq"), "head"),
            P(("grp", "seq"), "head"),
            P("head"),
            P("head"),
            P("head"),
            P("head", "seq"),
            P(("grp", "seq", "head"), None),
            P(),
            P(),
            P(("grp", "seq", "head"), None),
            P(("seq", "head"), None, None),
            P(("seq", "head"), None, None),
        ),
        out_specs=P(("grp", "seq", "head"), None),
        check_vma=False,
    )
```

```python
import functools
import jax
import jax.numpy as jnp
from jax import lax
from jax.experimental import pallas as pl
from jax.experimental.pallas import tpu as pltpu
from jax.sharding import PartitionSpec as P

HEADS = 64
HEAD_DIM = 64
STATE = 128
TOP = 6


EPSILON = 1e-05
ROUTE_SCALE = 2.5
MESH = pl.DeviceIdType.MESH


def mixer_kernel(
    pairs, heads_mesh, value_hbm, gate_hbm, write_hbm, read_hbm, step_t_ref, rate_ref, skip_ref,
    gain_ref, weight_hbm, out_ref,
    value_ref, gate_ref, write_ref, read_ref, cum_ref, cum_t_ref, coef_ref, ecum_ref, decay_ref,
    blocks, fresh, y_send, y_got, z_send, z_got, carry, mixed, normed, prod, sums,
    loads, su, sd, sy, rw, s_state, r_state, ss, rs,
):
    seq, head = lax.axis_index("seq"), lax.axis_index("head")
    z, y = seq // 2, seq % 2
    mate = {"seq": 2 * z + 1 - y}
    above, below = {"seq": seq + 2}, {"seq": seq - 2}
    heads, count = step_t_ref.shape
    groups = write_hbm.shape[1] // STATE
    per_group = heads // groups
    lanes = per_group * HEAD_DIM
    columns = weight_hbm.shape[0]
    pieces = 3 if columns % 48 == 0 else 1
    piece = columns // pieces
    own_rows = count // heads_mesh
    flat = heads * HEAD_DIM

    def remote(src, dst, send, recv, device):
        return pltpu.make_async_remote_copy(
            src_ref=src, dst_ref=dst, send_sem=send, recv_sem=recv,
            device_id=device, device_id_type=MESH,
        )

    def got(dst, sem):
        pltpu.make_async_copy(dst, dst, sem).wait()

    barrier = pltpu.get_barrier_semaphore()

    def greet(device):
        pl.semaphore_signal(barrier, inc=1, device_id=device, device_id_type=MESH)

    greet(mate)
    for j in range(1, heads_mesh):
        greet({"head": (head + j) % heads_mesh})

    @pl.when(z < pairs - 1)
    def _():
        greet(above)

    @pl.when(z > 0)
    def _():
        greet(below)

    copies = [
        pltpu.make_async_copy(there, here, loads.at[i])
        for i, (there, here) in enumerate(
            (
                (value_hbm, value_ref), (write_hbm, write_ref), (read_hbm, read_ref),
                (gate_hbm, gate_ref), (weight_hbm, blocks.at[seq]),
            )
        )
    ]
    for copy in copies:
        copy.start()
    ends = jnp.where(z < pairs - 1, 1, 0) + jnp.where(z > 0, 1, 0)
    pl.semaphore_wait(barrier, heads_mesh + ends)

    def piece_of(source, i):
        return blocks.at[source, pl.ds(i * piece, piece)]

    def weight_copy(source, i, sems, device):
        here = piece_of(source, i)
        return remote(here, here, sems.at[source, i], rw.at[source, i], device)

    def own_copy(i, sems, device):
        return remote(
            weight_hbm.at[pl.ds(i * piece, piece)], piece_of(seq, i), sems.at[seq, i],
            rw.at[seq, i], device,
        )

    @pl.when(z < pairs - 1)
    def _():
        for i in range(pieces):
            own_copy(i, su, above).start()

    @pl.when(z > 0)
    def _():
        for i in range(pieces):
            own_copy(i, sd, below).start()

    causal = lax.broadcasted_iota(jnp.int32, (count, count), 0) >= lax.broadcasted_iota(
        jnp.int32, (count, count), 1
    )
    diagonal = lax.broadcasted_iota(jnp.int32, (count, count), 0) == lax.broadcasted_iota(
        jnp.int32, (count, count), 1
    )

    def sums_of(a, b):
        return lax.dot_general(
            a, b, (((1,), (1,)), ((), ())), precision=lax.Precision.HIGHEST,
            preferred_element_type=jnp.float32,
        )

    triangle = jnp.where(causal, 1.0, 0.0)
    log_decay = -step_t_ref[...] * rate_ref[...]
    cumulative = sums_of(triangle, log_decay)
    steps = sums_of(jnp.where(diagonal, 1.0, 0.0), step_t_ref[...])
    cum_ref[...] = cumulative
    cum_t_ref[...] = sums_of(log_decay, triangle)
    coef_ref[...] = jnp.exp(cumulative[count - 1 :] - cumulative) * steps
    ecum_ref[...] = jnp.exp(cumulative)
    decay_ref[...] = jnp.zeros_like(decay_ref)
    decay_ref[:heads] = jnp.broadcast_to(
        jnp.exp(cum_t_ref[:, count - 1 : count]), (heads, STATE)
    )
    copies[0].wait()
    copies[1].wait()

    low = lax.broadcasted_iota(jnp.int32, (count, 2 * HEAD_DIM), 1) < HEAD_DIM

    def two_heads(ref, h):
        return jnp.where(low, ref[:, h : h + 1], ref[:, h + 1 : h + 2])

    for h in range(0, heads, 2):
        g = h // per_group
        at = slice(h * HEAD_DIM, (h + 2) * HEAD_DIM)
        weighted = (value_ref[:, at].astype(jnp.float32) * two_heads(coef_ref, h)).astype(
            jnp.bfloat16
        )
        fresh[at, :] = lax.dot_general(
            weighted, write_ref[:, g * STATE : (g + 1) * STATE], (((0,), (0,)), ((), ())),
            preferred_element_type=jnp.float32,
        )
    y_send[:flat] = fresh[...].astype(jnp.bfloat16)
    y_send[flat:] = decay_ref[...].astype(jnp.bfloat16)
    state_y = remote(y_send, y_got, s_state.at[0], r_state.at[0], mate)
    state_y.start()
    for i in range(pieces):
        own_copy(i, sy, mate).start()
    copies[2].wait()

    def inner(g):
        where = slice(g * STATE, (g + 1) * STATE)
        scores = lax.dot_general(
            read_ref[:, where], write_ref[:, where], (((1,), (1,)), ((), ())),
            preferred_element_type=jnp.float32,
        )
        for h in range(g * per_group, (g + 1) * per_group, 2):
            at = slice(h * HEAD_DIM, (h + 2) * HEAD_DIM)
            sides = []
            for n in (h, h + 1):
                decays = jnp.exp(
                    jnp.where(causal, cum_ref[:, n : n + 1] - cum_t_ref[n : n + 1, :], 0.0)
                )
                mixing = jnp.where(causal, scores * decays * step_t_ref[n : n + 1, :], 0.0)
                sides.append(
                    jnp.dot(
                        mixing.astype(jnp.bfloat16), value_ref[:, at],
                        preferred_element_type=jnp.float32,
                    )
                )
            mixed[:, at] = jnp.where(low, sides[0], sides[1]) + skip_ref[
                :, at
            ] * value_ref[:, at].astype(jnp.float32)

    def spread(decay):
        wide = jnp.broadcast_to(decay[:heads, None, :], (heads, HEAD_DIM, STATE))
        return wide.reshape(flat, STATE)

    def relay(k):
        for valid, onward, source, sems, device in (
            (z >= k, z < pairs - 1, seq - 2 * k, su, above),
            (z + k < pairs, z > 0, seq + 2 * k, sd, below),
        ):

            @pl.when(valid)
            def _(onward=onward, source=source, sems=sems, device=device):
                for i in range(pieces):
                    got(piece_of(source, i), rw.at[source, i])

                    @pl.when(onward)
                    def _():
                        weight_copy(source, i, sems, device).start()

                    weight_copy(source, i, sy, mate).start()

    inner(0)
    state_y.wait()
    theirs = y_got[:flat].astype(jnp.float32)
    their_decay = spread(y_got[flat:].astype(jnp.float32))
    my_decay = spread(decay_ref[...])
    pair_state = jnp.where(
        y == 1, my_decay * theirs + fresh[...], their_decay * fresh[...] + theirs
    )
    state_z = remote(z_send, z_got, s_state.at[1], r_state.at[1], above)

    @pl.when(z == 0)
    def _():
        z_send[...] = pair_state.astype(jnp.bfloat16)
        z_got[...] = jnp.zeros_like(z_got)
        state_z.start()

    for g in range(1, groups):
        inner(g)
    relay(1)

    @pl.when(z > 0)
    def _():
        got(z_got, r_state.at[1])

        @pl.when(z < pairs - 1)
        def _():
            z_send[...] = (
                my_decay * their_decay * z_got[...].astype(jnp.float32) + pair_state
            ).astype(jnp.bfloat16)
            state_z.start()

    entered = z_got[...].astype(jnp.float32)
    carry[...] = jnp.where(y == 1, their_decay * entered + theirs, entered).astype(jnp.bfloat16)
    copies[3].wait()
    for g in range(groups):
        at = slice(g * lanes, (g + 1) * lanes)
        carried = lax.dot_general(
            read_ref[:, g * STATE : (g + 1) * STATE], carry[at, :], (((1,), (1,)), ((), ())),
            preferred_element_type=jnp.float32,
        )
        scale = jnp.concatenate(
            [two_heads(ecum_ref, h) for h in range(g * per_group, (g + 1) * per_group, 2)], axis=1
        )
        gate = gate_ref[:, at].astype(jnp.float32)
        gated = (mixed[:, at] + carried * scale) * (gate * jax.nn.sigmoid(gate))
        inv_rms = lax.rsqrt(jnp.mean(gated * gated, axis=-1, keepdims=True) + EPSILON)
        normed[:, at] = (gated * inv_rms * gain_ref[:, at]).astype(jnp.bfloat16)

    def chunk_of(source, to):
        rows = pl.ds(pl.multiple_of(to * own_rows, own_rows), own_rows)
        return prod.at[source, rows]

    def give(source, to):
        return remote(
            chunk_of(source, to), sums.at[source, head], ss.at[source, to], rs.at[source, head],
            {"head": to},
        )

    def project(source):
        prod[source, :, pl.ds(0, columns)] = lax.dot_general(
            normed[...], blocks[source], (((1,), (1,)), ((), ())),
            preferred_element_type=jnp.float32,
        ).astype(jnp.bfloat16)
        for j in range(1, heads_mesh):
            give(source, (head + j) % heads_mesh).start()

    def arrived(source):
        for i in range(pieces):
            got(piece_of(source, i), rw.at[source, i])

    across = 1 - 2 * y
    prod[...] = jnp.zeros_like(prod)
    copies[4].wait()
    project(seq)
    for k in range(1, pairs):
        if k > 1:
            relay(k)
        if k == 1:
            arrived(seq + across)
            project(seq + across)
        for valid, source in ((z >= k, seq - 2 * k), (z + k < pairs, seq + 2 * k)):

            @pl.when(valid)
            def _(source=source):
                project(source)

        for valid, source in ((z >= k, seq - 2 * k), (z + k < pairs, seq + 2 * k)):

            @pl.when(valid)
            def _(source=source):
                arrived(source + across)
                project(source + across)

    def collect(source, carry_on):
        rows = pl.ds(pl.multiple_of(head * own_rows, own_rows), own_rows)
        total = prod[source, rows].astype(jnp.float32)
        for j in range(1, heads_mesh):
            other = (head + j) % heads_mesh
            got(sums.at[source, other], rs.at[source, other])
            total += sums[source, other].astype(jnp.float32)
        out_ref[source] = total
        return carry_on

    lax.fori_loop(0, 2 * pairs, collect, 0)

    @pl.when(z < pairs - 1)
    def _():
        state_z.wait_send()
        for i in range(pieces):
            own_copy(i, su, above).wait_send()

    @pl.when(z > 0)
    def _():
        for i in range(pieces):
            own_copy(i, sd, below).wait_send()

    for k in range(pairs):
        for valid, onward, source, sems, device in (
            (z >= k, z < pairs - 1, seq - 2 * k, su, above),
            (z + k < pairs, z > 0, seq + 2 * k, sd, below),
        ):
            if k == 0 and sems is sd:
                continue

            @pl.when(valid)
            def _(k=k, onward=onward, source=source, sems=sems, device=device):
                for i in range(pieces):
                    if k == 0:
                        own_copy(i, sy, mate).wait_send()
                    else:
                        weight_copy(source, i, sy, mate).wait_send()

                        @pl.when(onward)
                        def _():
                            weight_copy(source, i, sems, device).wait_send()

    def sent(source, carry_on):
        for j in range(1, heads_mesh):
            give(source, (head + j) % heads_mesh).wait_send()
        return carry_on

    lax.fori_loop(0, 2 * pairs, sent, 0)


def mixer(values, gates, writes, reads, steps, rates, skip_gain, norm_gain, weight):
    count, heads = steps.shape
    pairs, heads_mesh = lax.axis_size("seq") // 2, lax.axis_size("head")
    turned = weight.T
    columns, rows = turned.shape
    flat = heads * HEAD_DIM
    padded = -(-columns // 128) * 128
    pieces = 3 if columns % 48 == 0 else 1
    size = 2 * pairs
    dma = pltpu.SemaphoreType.DMA
    bf16 = jnp.bfloat16
    vmem = pl.BlockSpec(memory_space=pltpu.VMEM)
    anywhere = pl.BlockSpec(memory_space=pl.ANY)
    out = pl.pallas_call(
        functools.partial(mixer_kernel, pairs, heads_mesh),
        out_shape=jax.ShapeDtypeStruct((size, count // heads_mesh, padded), jnp.float32),
        in_specs=[anywhere] * 4 + [vmem] * 4 + [anywhere],
        out_specs=vmem,
        scratch_shapes=[
            pltpu.VMEM(values.shape, bf16),
            pltpu.VMEM(gates.shape, bf16),
            pltpu.VMEM(writes.shape, bf16),
            pltpu.VMEM(reads.shape, bf16),
            pltpu.VMEM((count, heads), jnp.float32),
            pltpu.VMEM((heads, count), jnp.float32),
            pltpu.VMEM((count, heads), jnp.float32),
            pltpu.VMEM((count, heads), jnp.float32),
            pltpu.VMEM((16, STATE), jnp.float32),
            pltpu.VMEM((size, columns, rows), bf16),
            pltpu.VMEM((flat, STATE), jnp.float32),
            pltpu.VMEM((flat + 16, STATE), bf16),
            pltpu.VMEM((flat + 16, STATE), bf16),
            pltpu.VMEM((flat, STATE), bf16),
            pltpu.VMEM((flat, STATE), bf16),
            pltpu.VMEM((flat, STATE), bf16),
            pltpu.VMEM((count, flat), jnp.float32),
            pltpu.VMEM((count, flat), bf16),
            pltpu.VMEM((size, count, padded), bf16),
            pltpu.VMEM((size, heads_mesh, count // heads_mesh, padded), bf16),
            dma((5,)),
            dma((size, pieces)), dma((size, pieces)), dma((size, pieces)), dma((size, pieces)),
            dma((2,)), dma((2,)),
            dma((size, heads_mesh)), dma((size, heads_mesh)),
        ],
        compiler_params=pltpu.CompilerParams(
            collective_id=0, has_side_effects=True, vmem_limit_bytes=48 * 1024 * 1024
        ),
    )(
        values, gates, writes, reads, steps.T, rates[:, None],
        jnp.repeat(skip_gain, HEAD_DIM)[None], norm_gain[None], turned,
    )
    return out[:, :, :columns].transpose(1, 0, 2).reshape(count // heads_mesh, size * columns)


def moe_kernel(
    planes, cols, cap, x_ref, info_ref, hidden_ref, up_hbm, down_hbm, out_ref,
    up, down, xz, iz, pk, rows, act, own, other, back, rb, pt, fin, total,
    weight_sem, sx_up, sx_down, rx, si, ri, sp, rp, sf, rf, sb, rbk, sr, rr, sn, rn,
):
    seq, head = lax.axis_index("seq"), lax.axis_index("head")
    wide = cols // 2
    z, y, x, c = seq // 2, seq % 2, head // 2, head % 2
    k = y * wide + x
    count, width = x_ref.shape
    tile = width // 7 if width % (7 * 128) == 0 else width
    deep = width // 3 if width % (3 * 128) == 0 else width
    slots = cols * cap

    def in_plane(col):
        return {"seq": 2 * z + col // wide, "head": 2 * (col % wide) + c}

    def in_line(plane):
        return {"seq": 2 * plane + y, "head": head}

    mate = {"seq": seq, "head": 2 * x + 1 - c}

    def remote(src, dst, send, recv, device):
        return pltpu.make_async_remote_copy(
            src_ref=src, dst_ref=dst, send_sem=send, recv_sem=recv,
            device_id=device, device_id_type=MESH,
        )

    xz[z] = x_ref[...]
    load_up = pltpu.make_async_copy(up_hbm.at[0], up, weight_sem.at[0])
    load_down = pltpu.make_async_copy(down_hbm.at[0], down, weight_sem.at[1])
    load_up.start()
    load_down.start()

    barrier = pltpu.get_barrier_semaphore()
    for d in range(1, planes):
        pl.semaphore_signal(
            barrier, inc=1, device_id=in_line((z + d) % planes), device_id_type=MESH
        )
    for j in range(1, cols):
        pl.semaphore_signal(
            barrier, inc=1, device_id=in_plane((k + j) % cols), device_id_type=MESH
        )
    pl.semaphore_signal(barrier, inc=1, device_id=mate, device_id_type=MESH)
    pl.semaphore_wait(barrier, planes + cols - 1)

    def line_rows(block, sems, to):
        return remote(xz.at[block], xz.at[block], sems.at[block], rx.at[block], in_line(to))

    def line_info(to):
        return remote(info_ref.at[to], iz.at[z], si.at[to], ri.at[z], in_line(to))

    def spread(block, col):
        part = pl.ds(pl.multiple_of(col * cap, cap), cap)
        place = pl.ds(pl.multiple_of(k * cap, cap), cap)
        return remote(
            pk.at[block, part], rows.at[block, 0, place],
            sp.at[block, col], rp.at[block, k], in_plane(col),
        )

    def forward(block):
        return remote(rows.at[block, 0], rows.at[block, 1], sf.at[block], rf.at[block], mate)

    def half_back(block):
        return remote(other.at[block], back.at[block], sb.at[block], rbk.at[block], mate)

    def give_back(block, col):
        part = pl.ds(pl.multiple_of(col * cap, cap), cap)
        place = pl.ds(pl.multiple_of(k * cap, cap), cap)
        return remote(
            own.at[block, part], rb.at[block, place],
            sr.at[block, col], rr.at[block, k], in_plane(col),
        )

    def line_back(to):
        return remote(pt.at[to], fin.at[z], sn.at[to], rn.at[z], in_line(to))

    def got(dst, sem):
        pltpu.make_async_copy(dst, dst, sem).wait()

    def source(d):
        near = jnp.minimum(z, planes - 1 - z)
        sign = jnp.where(d % 2 == 1, -1, 1)
        far = jnp.where(z == near, z + (d - near), z - (d - near))
        return jnp.where(d <= 2 * near, z + sign * ((d + 1) // 2), far)

    def onward(block, act):
        @pl.when((block <= z) & (z < planes - 1))
        def _():
            act(line_rows(block, sx_up, z + 1))

        @pl.when((block >= z) & (z > 0))
        def _():
            act(line_rows(block, sx_down, z - 1))

    onward(z, lambda copy: copy.start())
    for d in range(1, planes):
        line_info((z + d) % planes).start()

    mine = pl.ds(pl.multiple_of(k * cap, cap), cap)

    def pack(d):
        block = source(d)

        @pl.when(d == 0)
        def _():
            iz[z] = info_ref[z]

        @pl.when(d > 0)
        def _():
            got(xz.at[block], rx.at[block])
            onward(block, lambda copy: copy.start())
            got(iz.at[block], ri.at[block])

        pk[block] = lax.dot_general(
            iz[block, pl.ds(0, count)], xz[block], (((0,), (0,)), ((), ())),
            preferred_element_type=jnp.float32,
        ).astype(jnp.bfloat16)
        for j in range(1, cols):
            spread(block, (k + j) % cols).start()
        rows[block, 0, mine] = pk[block, mine]

    def pass_on(d):
        block = source(d)
        for j in range(1, cols):
            col = (k + j) % cols
            place = pl.ds(pl.multiple_of(col * cap, cap), cap)
            got(rows.at[block, 0, place], rp.at[block, col])
        forward(block).start()

    def compute(d):
        block = source(d)

        @pl.when(d == 0)
        def _():
            load_up.wait()
            load_down.wait()

        got(rows.at[block, 1], rf.at[block])
        total[...] = jnp.zeros_like(total)

        def gather_up(i, carry):
            at = pl.ds(pl.multiple_of(i * deep, 128), deep)
            taken = rows[block, :, :, at].reshape(2 * slots, deep)
            total[...] += lax.dot_general(
                taken, up[:, at], (((1,), (1,)), ((), ())), preferred_element_type=jnp.float32
            )
            return carry

        lax.fori_loop(0, width // deep, gather_up, 0)
        kept = jnp.maximum(total[...], 0.0)
        act[...] = (kept * kept).astype(jnp.bfloat16)

        def gather_down(i, carry):
            at = pl.ds(pl.multiple_of(i * tile, 128), tile)
            result = jnp.dot(act[...], down[:, at], preferred_element_type=jnp.float32)
            result = result.astype(jnp.bfloat16)
            own[block, :, at] = result[:slots]
            other[block, :, at] = result[slots:]
            return carry

        lax.fori_loop(0, width // tile, gather_down, 0)
        half_back(block).start()

    def add_halves(d):
        block = source(d)
        got(back.at[block], rbk.at[block])
        own[block] = (
            own[block].astype(jnp.float32) + back[block].astype(jnp.float32)
        ).astype(jnp.bfloat16)
        for j in range(1, cols):
            give_back(block, (k + j) % cols).start()
        rb[block, mine] = own[block, mine]

    def combine(d):
        block = source(d)
        for j in range(1, cols):
            col = (k + j) % cols
            place = pl.ds(pl.multiple_of(col * cap, cap), cap)
            got(rb.at[block, place], rr.at[block, col])
        pt[block] = jnp.dot(
            iz[block, pl.ds(count, count)], rb[block], preferred_element_type=jnp.float32
        ).astype(jnp.bfloat16)

        @pl.when(d > 0)
        def _():
            line_back(block).start()

    def step(t, carry):
        for lag, stage in ((0, pack), (1, pass_on), (2, add_halves), (1, compute), (3, combine)):

            @pl.when((t >= lag) & (t < planes + lag))
            def _(lag=lag, stage=stage):
                stage(t - lag)

        return carry

    lax.fori_loop(0, planes + 3, step, 0)

    answer = hidden_ref[...] + pt[z].astype(jnp.float32)
    for d in range(1, planes):
        block = (z + planes - d) % planes
        got(fin.at[block], rn.at[block])
        answer += fin[block].astype(jnp.float32)
    out_ref[...] = answer.astype(out_ref.dtype)

    for d in range(1, planes):
        to = (z + d) % planes
        line_info(to).wait_send()
        line_back(to).wait_send()

    def finish(block, carry):
        for j in range(1, cols):
            spread(block, (k + j) % cols).wait_send()
            give_back(block, (k + j) % cols).wait_send()
        onward(block, lambda copy: copy.wait_send())
        forward(block).wait_send()
        half_back(block).wait_send()
        return carry

    lax.fori_loop(0, planes, finish, 0)


def expert_layer(inputs, info, hidden, up_weight, down_weight, planes, cols, cap):
    count, width = inputs.shape
    units = up_weight.shape[2]
    slots = cols * cap
    dma = pltpu.SemaphoreType.DMA
    bf16 = jnp.bfloat16
    vmem = pl.BlockSpec(memory_space=pltpu.VMEM)
    return pl.pallas_call(
        functools.partial(moe_kernel, planes, cols, cap),
        out_shape=jax.ShapeDtypeStruct((count, width), bf16),
        in_specs=[vmem, vmem, vmem, pl.BlockSpec(memory_space=pl.ANY), pl.BlockSpec(memory_space=pl.ANY)],
        out_specs=vmem,
        scratch_shapes=[
            pltpu.VMEM((units, width), bf16),
            pltpu.VMEM((units, width), bf16),
            pltpu.VMEM((planes, count, width), bf16),
            pltpu.VMEM((planes, 2 * count, slots), bf16),
            pltpu.VMEM((planes, slots, width), bf16),
            pltpu.VMEM((planes, 2, slots, width), bf16),
            pltpu.VMEM((2 * slots, units), bf16),
            pltpu.VMEM((planes, slots, width), bf16),
            pltpu.VMEM((planes, slots, width), bf16),
            pltpu.VMEM((planes, slots, width), bf16),
            pltpu.VMEM((planes, slots, width), bf16),
            pltpu.VMEM((planes, count, width), bf16),
            pltpu.VMEM((planes, count, width), bf16),
            pltpu.VMEM((2 * slots, units), jnp.float32),
            dma((2,)),
            dma((planes,)), dma((planes,)), dma((planes,)), dma((planes,)), dma((planes,)),
            dma((planes, cols)), dma((planes, cols)),
            dma((planes,)), dma((planes,)), dma((planes,)), dma((planes,)),
            dma((planes, cols)), dma((planes, cols)),
            dma((planes,)), dma((planes,)),
        ],
        compiler_params=pltpu.CompilerParams(
            collective_id=1, has_side_effects=True, vmem_limit_bytes=60 * 1024 * 1024
        ),
        cost_estimate=pl.CostEstimate(
            flops=8 * planes * slots * width * units,
            bytes_accessed=4 * width * units,
            transcendentals=0,
        ),
    )(inputs, info, hidden, up_weight.swapaxes(1, 2), down_weight)


def per_device(
    ssm_values,
    ssm_gate,
    write_proj,
    read_proj,
    step_size,
    decay_power,
    skip_gain,
    norm_gain,
    out_weight,
    residual,
    expert_norm,
    router_weight,
    expert_index,
    up_weight,
    down_weight,
):
    tokens_dev = ssm_values.shape[0]
    decay_rates = jnp.exp2(-decay_power.astype(jnp.float32))
    mixed_out = mixer(
        ssm_values, ssm_gate, write_proj, read_proj, step_size, decay_rates, skip_gain, norm_gain,
        out_weight,
    )
    rows_own = tokens_dev // lax.axis_size("head")
    hidden = residual.astype(jnp.float32) + mixed_out
    inputs = (
        hidden
        * lax.rsqrt(jnp.mean(hidden * hidden, axis=-1, keepdims=True) + EPSILON)
        * expert_norm[None, :]
    ).astype(jnp.bfloat16)
    logits = jnp.dot(inputs, router_weight, preferred_element_type=jnp.float32)
    experts = router_weight.shape[1]
    model_width = inputs.shape[1]
    expert_hits = expert_index[:, :, None] == jnp.arange(experts, dtype=jnp.int32)[None, None, :]
    picked = jnp.sum(jnp.where(expert_hits, logits[:, None, :], 0.0), axis=-1)
    probability = jax.nn.sigmoid(picked)
    shares = ROUTE_SCALE * probability / jnp.sum(probability, axis=1, keepdims=True)
    capacity = (
        8
        * TOP
        * tokens_dev
        // (3 * lax.axis_size("seq") * lax.axis_size("head") * lax.axis_size("head"))
    )
    flat_hits = expert_hits.astype(jnp.int32).reshape(rows_own * TOP, experts)
    before = jnp.cumsum(flat_hits, axis=0) - flat_hits
    slot_index = jnp.sum(before * flat_hits, axis=1)
    cols = lax.axis_size("head")
    planes = lax.axis_size("seq") // 2
    cap = -(-capacity // 16) * 16
    target = expert_index * cap + slot_index.reshape(rows_own, TOP)
    chosen = target[:, :, None] == jnp.arange(experts * cap, dtype=jnp.int32)[None, None, :]
    place = jnp.any(chosen, axis=1).astype(jnp.bfloat16)
    weigh = jnp.sum(jnp.where(chosen, shares[:, :, None], 0.0), axis=1).astype(jnp.bfloat16)
    info = jnp.concatenate([place, weigh], axis=0)
    info = info.reshape(2 * rows_own, planes, cols * cap).transpose(1, 0, 2)
    return expert_layer(inputs, info, hidden, up_weight, down_weight, planes, cols, cap)


def solution(mesh):
    return jax.shard_map(
        per_device,
        mesh=mesh,
        in_specs=(
            P(("grp", "seq"), "head"),
            P(("grp", "seq"), "head"),
            P(("grp", "seq"), "head"),
            P(("grp", "seq"), "head"),
            P(("grp", "seq"), "head"),
            P("head"),
            P("head"),
            P("head"),
            P("head", "seq"),
            P(("grp", "seq", "head"), None),
            P(),
            P(),
            P(("grp", "seq", "head"), None),
            P(("seq", "head"), None, None),
            P(("seq", "head"), None, None),
        ),
        out_specs=P(("grp", "seq", "head"), None),
        check_vma=False,
    )
```

```python
import functools
import jax
import jax.numpy as jnp
from jax import lax
from jax.experimental import pallas as pl
from jax.experimental.pallas import tpu as pltpu
from jax.sharding import PartitionSpec as P

HEADS = 64
HEAD_DIM = 64
STATE = 128
TOP = 6


EPSILON = 1e-05
ROUTE_SCALE = 2.5
MESH = pl.DeviceIdType.MESH


def mixer_kernel(
    pairs, heads_mesh, value_hbm, gate_hbm, write_hbm, read_hbm, step_t_ref, rate_ref, skip_ref,
    gain_ref, weight_hbm, out_ref,
    value_ref, gate_ref, write_ref, read_ref, cum_ref, cum_t_ref, coef_ref, ecum_ref, decay_ref,
    blocks, fresh, y_send, y_got, z_send, z_got, carry, mixed, normed, prod, sums,
    loads, su, sd, sy, rw, s_state, r_state, ss, rs,
):
    seq, head = lax.axis_index("seq"), lax.axis_index("head")
    z, y = seq // 2, seq % 2
    mate = {"seq": 2 * z + 1 - y}
    above, below = {"seq": seq + 2}, {"seq": seq - 2}
    heads, count = step_t_ref.shape
    groups = write_hbm.shape[1] // STATE
    per_group = heads // groups
    lanes = per_group * HEAD_DIM
    columns = weight_hbm.shape[0]
    pieces = 3 if columns % 48 == 0 else 1
    piece = columns // pieces
    own_rows = count // heads_mesh
    flat = heads * HEAD_DIM

    def remote(src, dst, send, recv, device):
        return pltpu.make_async_remote_copy(
            src_ref=src, dst_ref=dst, send_sem=send, recv_sem=recv,
            device_id=device, device_id_type=MESH,
        )

    def got(dst, sem):
        pltpu.make_async_copy(dst, dst, sem).wait()

    barrier = pltpu.get_barrier_semaphore()

    def greet(device):
        pl.semaphore_signal(barrier, inc=1, device_id=device, device_id_type=MESH)

    greet(mate)
    for j in range(1, heads_mesh):
        greet({"head": (head + j) % heads_mesh})

    @pl.when(z < pairs - 1)
    def _():
        greet(above)

    @pl.when(z > 0)
    def _():
        greet(below)

    copies = [
        pltpu.make_async_copy(there, here, loads.at[i])
        for i, (there, here) in enumerate(
            (
                (value_hbm, value_ref), (write_hbm, write_ref), (read_hbm, read_ref),
                (gate_hbm, gate_ref), (weight_hbm, blocks.at[seq]),
            )
        )
    ]
    for copy in copies:
        copy.start()
    ends = jnp.where(z < pairs - 1, 1, 0) + jnp.where(z > 0, 1, 0)
    pl.semaphore_wait(barrier, heads_mesh + ends)

    def piece_of(source, i):
        return blocks.at[source, pl.ds(i * piece, piece)]

    def weight_copy(source, i, sems, device):
        here = piece_of(source, i)
        return remote(here, here, sems.at[source, i], rw.at[source, i], device)

    def own_copy(i, sems, device):
        return remote(
            weight_hbm.at[pl.ds(i * piece, piece)], piece_of(seq, i), sems.at[seq, i],
            rw.at[seq, i], device,
        )

    @pl.when(z < pairs - 1)
    def _():
        for i in range(pieces):
            own_copy(i, su, above).start()

    @pl.when(z > 0)
    def _():
        for i in range(pieces):
            own_copy(i, sd, below).start()

    causal = lax.broadcasted_iota(jnp.int32, (count, count), 0) >= lax.broadcasted_iota(
        jnp.int32, (count, count), 1
    )
    diagonal = lax.broadcasted_iota(jnp.int32, (count, count), 0) == lax.broadcasted_iota(
        jnp.int32, (count, count), 1
    )

    def sums_of(a, b):
        return lax.dot_general(
            a, b, (((1,), (1,)), ((), ())), precision=lax.Precision.HIGHEST,
            preferred_element_type=jnp.float32,
        )

    triangle = jnp.where(causal, 1.0, 0.0)
    log_decay = -step_t_ref[...] * rate_ref[...]
    cumulative = sums_of(triangle, log_decay)
    steps = sums_of(jnp.where(diagonal, 1.0, 0.0), step_t_ref[...])
    cum_ref[...] = cumulative
    cum_t_ref[...] = sums_of(log_decay, triangle)
    coef_ref[...] = jnp.exp(cumulative[count - 1 :] - cumulative) * steps
    ecum_ref[...] = jnp.exp(cumulative)
    decay_ref[...] = jnp.zeros_like(decay_ref)
    decay_ref[:heads] = jnp.broadcast_to(
        jnp.exp(cum_t_ref[:, count - 1 : count]), (heads, STATE)
    )
    copies[0].wait()
    copies[1].wait()

    low = lax.broadcasted_iota(jnp.int32, (count, 2 * HEAD_DIM), 1) < HEAD_DIM

    def two_heads(ref, h):
        return jnp.where(low, ref[:, h : h + 1], ref[:, h + 1 : h + 2])

    for h in range(0, heads, 2):
        g = h // per_group
        at = slice(h * HEAD_DIM, (h + 2) * HEAD_DIM)
        weighted = (value_ref[:, at].astype(jnp.float32) * two_heads(coef_ref, h)).astype(
            jnp.bfloat16
        )
        fresh[at, :] = lax.dot_general(
            weighted, write_ref[:, g * STATE : (g + 1) * STATE], (((0,), (0,)), ((), ())),
            preferred_element_type=jnp.float32,
        )
    y_send[:flat] = fresh[...].astype(jnp.bfloat16)
    y_send[flat:] = decay_ref[...].astype(jnp.bfloat16)
    state_y = remote(y_send, y_got, s_state.at[0], r_state.at[0], mate)
    state_y.start()
    for i in range(pieces):
        own_copy(i, sy, mate).start()
    copies[2].wait()

    def inner(g):
        where = slice(g * STATE, (g + 1) * STATE)
        scores = lax.dot_general(
            read_ref[:, where], write_ref[:, where], (((1,), (1,)), ((), ())),
            preferred_element_type=jnp.float32,
        )
        for h in range(g * per_group, (g + 1) * per_group, 2):
            at = slice(h * HEAD_DIM, (h + 2) * HEAD_DIM)
            sides = []
            for n in (h, h + 1):
                decays = jnp.exp(
                    jnp.where(causal, cum_ref[:, n : n + 1] - cum_t_ref[n : n + 1, :], 0.0)
                )
                mixing = jnp.where(causal, scores * decays * step_t_ref[n : n + 1, :], 0.0)
                sides.append(
                    jnp.dot(
                        mixing.astype(jnp.bfloat16), value_ref[:, at],
                        preferred_element_type=jnp.float32,
                    )
                )
            mixed[:, at] = jnp.where(low, sides[0], sides[1]) + skip_ref[
                :, at
            ] * value_ref[:, at].astype(jnp.float32)

    def spread(decay):
        wide = jnp.broadcast_to(decay[:heads, None, :], (heads, HEAD_DIM, STATE))
        return wide.reshape(flat, STATE)

    def relay(k):
        for valid, onward, source, sems, device in (
            (z >= k, z < pairs - 1, seq - 2 * k, su, above),
            (z + k < pairs, z > 0, seq + 2 * k, sd, below),
        ):

            @pl.when(valid)
            def _(onward=onward, source=source, sems=sems, device=device):
                for i in range(pieces):
                    got(piece_of(source, i), rw.at[source, i])

                    @pl.when(onward)
                    def _():
                        weight_copy(source, i, sems, device).start()

                    weight_copy(source, i, sy, mate).start()

    inner(0)
    state_y.wait()
    theirs = y_got[:flat].astype(jnp.float32)
    their_decay = spread(y_got[flat:].astype(jnp.float32))
    my_decay = spread(decay_ref[...])
    pair_state = jnp.where(
        y == 1, my_decay * theirs + fresh[...], their_decay * fresh[...] + theirs
    )
    state_z = remote(z_send, z_got, s_state.at[1], r_state.at[1], above)

    @pl.when(z == 0)
    def _():
        z_send[...] = pair_state.astype(jnp.bfloat16)
        z_got[...] = jnp.zeros_like(z_got)
        state_z.start()

    for g in range(1, groups):
        inner(g)
    relay(1)

    @pl.when(z > 0)
    def _():
        got(z_got, r_state.at[1])

        @pl.when(z < pairs - 1)
        def _():
            z_send[...] = (
                my_decay * their_decay * z_got[...].astype(jnp.float32) + pair_state
            ).astype(jnp.bfloat16)
            state_z.start()

    entered = z_got[...].astype(jnp.float32)
    carry[...] = jnp.where(y == 1, their_decay * entered + theirs, entered).astype(jnp.bfloat16)
    copies[3].wait()
    for g in range(groups):
        at = slice(g * lanes, (g + 1) * lanes)
        carried = lax.dot_general(
            read_ref[:, g * STATE : (g + 1) * STATE], carry[at, :], (((1,), (1,)), ((), ())),
            preferred_element_type=jnp.float32,
        )
        scale = jnp.concatenate(
            [two_heads(ecum_ref, h) for h in range(g * per_group, (g + 1) * per_group, 2)], axis=1
        )
        gate = gate_ref[:, at].astype(jnp.float32)
        gated = (mixed[:, at] + carried * scale) * (gate * jax.nn.sigmoid(gate))
        inv_rms = lax.rsqrt(jnp.mean(gated * gated, axis=-1, keepdims=True) + EPSILON)
        normed[:, at] = (gated * inv_rms * gain_ref[:, at]).astype(jnp.bfloat16)

    def chunk_of(source, to):
        rows = pl.ds(pl.multiple_of(to * own_rows, own_rows), own_rows)
        return prod.at[source, rows]

    def give(source, to):
        return remote(
            chunk_of(source, to), sums.at[source, head], ss.at[source, to], rs.at[source, head],
            {"head": to},
        )

    def project(source):
        prod[source, :, pl.ds(0, columns)] = lax.dot_general(
            normed[...], blocks[source], (((1,), (1,)), ((), ())),
            preferred_element_type=jnp.float32,
        ).astype(jnp.bfloat16)
        for j in range(1, heads_mesh):
            give(source, (head + j) % heads_mesh).start()

    def arrived(source):
        for i in range(pieces):
            got(piece_of(source, i), rw.at[source, i])

    across = 1 - 2 * y
    prod[...] = jnp.zeros_like(prod)
    copies[4].wait()
    project(seq)
    for k in range(1, pairs):
        if k == 1:
            arrived(seq + across)
            project(seq + across)
        for valid, source in ((z >= k, seq - 2 * k), (z + k < pairs, seq + 2 * k)):

            @pl.when(valid)
            def _(source=source):
                project(source)

        if k + 1 < pairs:
            relay(k + 1)
        for valid, source in ((z >= k, seq - 2 * k), (z + k < pairs, seq + 2 * k)):

            @pl.when(valid)
            def _(source=source):
                arrived(source + across)
                project(source + across)

    def collect(source, carry_on):
        rows = pl.ds(pl.multiple_of(head * own_rows, own_rows), own_rows)
        total = prod[source, rows].astype(jnp.float32)
        for j in range(1, heads_mesh):
            other = (head + j) % heads_mesh
            got(sums.at[source, other], rs.at[source, other])
            total += sums[source, other].astype(jnp.float32)
        out_ref[source] = total
        return carry_on

    lax.fori_loop(0, 2 * pairs, collect, 0)

    @pl.when(z < pairs - 1)
    def _():
        state_z.wait_send()
        for i in range(pieces):
            own_copy(i, su, above).wait_send()

    @pl.when(z > 0)
    def _():
        for i in range(pieces):
            own_copy(i, sd, below).wait_send()

    for k in range(pairs):
        for valid, onward, source, sems, device in (
            (z >= k, z < pairs - 1, seq - 2 * k, su, above),
            (z + k < pairs, z > 0, seq + 2 * k, sd, below),
        ):
            if k == 0 and sems is sd:
                continue

            @pl.when(valid)
            def _(k=k, onward=onward, source=source, sems=sems, device=device):
                for i in range(pieces):
                    if k == 0:
                        own_copy(i, sy, mate).wait_send()
                    else:
                        weight_copy(source, i, sy, mate).wait_send()

                        @pl.when(onward)
                        def _():
                            weight_copy(source, i, sems, device).wait_send()

    def sent(source, carry_on):
        for j in range(1, heads_mesh):
            give(source, (head + j) % heads_mesh).wait_send()
        return carry_on

    lax.fori_loop(0, 2 * pairs, sent, 0)


def mixer(values, gates, writes, reads, steps, rates, skip_gain, norm_gain, weight):
    count, heads = steps.shape
    pairs, heads_mesh = lax.axis_size("seq") // 2, lax.axis_size("head")
    turned = weight.T
    columns, rows = turned.shape
    flat = heads * HEAD_DIM
    padded = -(-columns // 128) * 128
    pieces = 3 if columns % 48 == 0 else 1
    size = 2 * pairs
    dma = pltpu.SemaphoreType.DMA
    bf16 = jnp.bfloat16
    vmem = pl.BlockSpec(memory_space=pltpu.VMEM)
    anywhere = pl.BlockSpec(memory_space=pl.ANY)
    out = pl.pallas_call(
        functools.partial(mixer_kernel, pairs, heads_mesh),
        out_shape=jax.ShapeDtypeStruct((size, count // heads_mesh, padded), jnp.float32),
        in_specs=[anywhere] * 4 + [vmem] * 4 + [anywhere],
        out_specs=vmem,
        scratch_shapes=[
            pltpu.VMEM(values.shape, bf16),
            pltpu.VMEM(gates.shape, bf16),
            pltpu.VMEM(writes.shape, bf16),
            pltpu.VMEM(reads.shape, bf16),
            pltpu.VMEM((count, heads), jnp.float32),
            pltpu.VMEM((heads, count), jnp.float32),
            pltpu.VMEM((count, heads), jnp.float32),
            pltpu.VMEM((count, heads), jnp.float32),
            pltpu.VMEM((16, STATE), jnp.float32),
            pltpu.VMEM((size, columns, rows), bf16),
            pltpu.VMEM((flat, STATE), jnp.float32),
            pltpu.VMEM((flat + 16, STATE), bf16),
            pltpu.VMEM((flat + 16, STATE), bf16),
            pltpu.VMEM((flat, STATE), bf16),
            pltpu.VMEM((flat, STATE), bf16),
            pltpu.VMEM((flat, STATE), bf16),
            pltpu.VMEM((count, flat), jnp.float32),
            pltpu.VMEM((count, flat), bf16),
            pltpu.VMEM((size, count, padded), bf16),
            pltpu.VMEM((size, heads_mesh, count // heads_mesh, padded), bf16),
            dma((5,)),
            dma((size, pieces)), dma((size, pieces)), dma((size, pieces)), dma((size, pieces)),
            dma((2,)), dma((2,)),
            dma((size, heads_mesh)), dma((size, heads_mesh)),
        ],
        compiler_params=pltpu.CompilerParams(
            collective_id=0, has_side_effects=True, vmem_limit_bytes=62 * 1024 * 1024
        ),
    )(
        values, gates, writes, reads, steps.T, rates[:, None],
        jnp.repeat(skip_gain, HEAD_DIM)[None], norm_gain[None], turned,
    )
    return out[:, :, :columns].transpose(1, 0, 2).reshape(count // heads_mesh, size * columns)


def moe_kernel(
    planes, cols, cap, x_ref, info_ref, hidden_ref, up_hbm, down_hbm, out_ref,
    up, down, xz, iz, pk, rows, act, own, other, back, rb, pt, fin, total,
    weight_sem, sx_up, sx_down, rx, si, ri, sp, rp, sf, rf, sb, rbk, sr, rr, sn, rn,
):
    seq, head = lax.axis_index("seq"), lax.axis_index("head")
    wide = cols // 2
    z, y, x, c = seq // 2, seq % 2, head // 2, head % 2
    k = y * wide + x
    count, width = x_ref.shape
    tile = width // 7 if width % (7 * 128) == 0 else width
    deep = width // 3 if width % (3 * 128) == 0 else width
    slots = cols * cap

    def in_plane(col):
        return {"seq": 2 * z + col // wide, "head": 2 * (col % wide) + c}

    def in_line(plane):
        return {"seq": 2 * plane + y, "head": head}

    mate = {"seq": seq, "head": 2 * x + 1 - c}

    def remote(src, dst, send, recv, device):
        return pltpu.make_async_remote_copy(
            src_ref=src, dst_ref=dst, send_sem=send, recv_sem=recv,
            device_id=device, device_id_type=MESH,
        )

    xz[z] = x_ref[...]
    load_up = pltpu.make_async_copy(up_hbm.at[0], up, weight_sem.at[0])
    load_down = pltpu.make_async_copy(down_hbm.at[0], down, weight_sem.at[1])
    load_up.start()
    load_down.start()

    barrier = pltpu.get_barrier_semaphore()
    for d in range(1, planes):
        pl.semaphore_signal(
            barrier, inc=1, device_id=in_line((z + d) % planes), device_id_type=MESH
        )
    for j in range(1, cols):
        pl.semaphore_signal(
            barrier, inc=1, device_id=in_plane((k + j) % cols), device_id_type=MESH
        )
    pl.semaphore_signal(barrier, inc=1, device_id=mate, device_id_type=MESH)
    pl.semaphore_wait(barrier, planes + cols - 1)

    def line_rows(block, sems, to):
        return remote(xz.at[block], xz.at[block], sems.at[block], rx.at[block], in_line(to))

    def line_info(to):
        return remote(info_ref.at[to], iz.at[z], si.at[to], ri.at[z], in_line(to))

    def spread(block, col):
        part = pl.ds(pl.multiple_of(col * cap, cap), cap)
        place = pl.ds(pl.multiple_of(k * cap, cap), cap)
        return remote(
            pk.at[block, part], rows.at[block, 0, place],
            sp.at[block, col], rp.at[block, k], in_plane(col),
        )

    def forward(block):
        return remote(rows.at[block, 0], rows.at[block, 1], sf.at[block], rf.at[block], mate)

    def half_back(block):
        return remote(other.at[block], back.at[block], sb.at[block], rbk.at[block], mate)

    def give_back(block, col):
        part = pl.ds(pl.multiple_of(col * cap, cap), cap)
        place = pl.ds(pl.multiple_of(k * cap, cap), cap)
        return remote(
            own.at[block, part], rb.at[block, place],
            sr.at[block, col], rr.at[block, k], in_plane(col),
        )

    def line_back(to):
        return remote(pt.at[to], fin.at[z], sn.at[to], rn.at[z], in_line(to))

    def got(dst, sem):
        pltpu.make_async_copy(dst, dst, sem).wait()

    def source(d):
        near = jnp.minimum(z, planes - 1 - z)
        sign = jnp.where(d % 2 == 1, -1, 1)
        far = jnp.where(z == near, z + (d - near), z - (d - near))
        return jnp.where(d <= 2 * near, z + sign * ((d + 1) // 2), far)

    def onward(block, act):
        @pl.when((block <= z) & (z < planes - 1))
        def _():
            act(line_rows(block, sx_up, z + 1))

        @pl.when((block >= z) & (z > 0))
        def _():
            act(line_rows(block, sx_down, z - 1))

    onward(z, lambda copy: copy.start())
    for d in range(1, planes):
        line_info((z + d) % planes).start()

    mine = pl.ds(pl.multiple_of(k * cap, cap), cap)

    def pack(d):
        block = source(d)

        @pl.when(d == 0)
        def _():
            iz[z] = info_ref[z]

        @pl.when(d > 0)
        def _():
            got(xz.at[block], rx.at[block])
            onward(block, lambda copy: copy.start())
            got(iz.at[block], ri.at[block])

        pk[block] = lax.dot_general(
            iz[block, pl.ds(0, count)], xz[block], (((0,), (0,)), ((), ())),
            preferred_element_type=jnp.float32,
        ).astype(jnp.bfloat16)
        for j in range(1, cols):
            spread(block, (k + j) % cols).start()
        rows[block, 0, mine] = pk[block, mine]

    def pass_on(d):
        block = source(d)
        for j in range(1, cols):
            col = (k + j) % cols
            place = pl.ds(pl.multiple_of(col * cap, cap), cap)
            got(rows.at[block, 0, place], rp.at[block, col])
        forward(block).start()

    def compute(d):
        block = source(d)

        @pl.when(d == 0)
        def _():
            load_up.wait()
            load_down.wait()

        got(rows.at[block, 1], rf.at[block])
        total[...] = jnp.zeros_like(total)

        def gather_up(i, carry):
            at = pl.ds(pl.multiple_of(i * deep, 128), deep)
            taken = rows[block, :, :, at].reshape(2 * slots, deep)
            total[...] += lax.dot_general(
                taken, up[:, at], (((1,), (1,)), ((), ())), preferred_element_type=jnp.float32
            )
            return carry

        lax.fori_loop(0, width // deep, gather_up, 0)
        kept = jnp.maximum(total[...], 0.0)
        act[...] = (kept * kept).astype(jnp.bfloat16)

        def gather_down(i, carry):
            at = pl.ds(pl.multiple_of(i * tile, 128), tile)
            result = jnp.dot(act[...], down[:, at], preferred_element_type=jnp.float32)
            result = result.astype(jnp.bfloat16)
            own[block, :, at] = result[:slots]
            other[block, :, at] = result[slots:]
            return carry

        lax.fori_loop(0, width // tile, gather_down, 0)
        half_back(block).start()

    def add_halves(d):
        block = source(d)
        got(back.at[block], rbk.at[block])
        own[block] = (
            own[block].astype(jnp.float32) + back[block].astype(jnp.float32)
        ).astype(jnp.bfloat16)
        for j in range(1, cols):
            give_back(block, (k + j) % cols).start()
        rb[block, mine] = own[block, mine]

    def combine(d):
        block = source(d)
        for j in range(1, cols):
            col = (k + j) % cols
            place = pl.ds(pl.multiple_of(col * cap, cap), cap)
            got(rb.at[block, place], rr.at[block, col])
        pt[block] = jnp.dot(
            iz[block, pl.ds(count, count)], rb[block], preferred_element_type=jnp.float32
        ).astype(jnp.bfloat16)

        @pl.when(d > 0)
        def _():
            line_back(block).start()

    def step(t, carry):
        for lag, stage in ((0, pack), (1, pass_on), (2, add_halves), (3, combine), (1, compute)):

            @pl.when((t >= lag) & (t < planes + lag))
            def _(lag=lag, stage=stage):
                stage(t - lag)

        return carry

    lax.fori_loop(0, planes + 3, step, 0)

    answer = hidden_ref[...] + pt[z].astype(jnp.float32)
    for d in range(1, planes):
        block = (z + planes - d) % planes
        got(fin.at[block], rn.at[block])
        answer += fin[block].astype(jnp.float32)
    out_ref[...] = answer.astype(out_ref.dtype)

    for d in range(1, planes):
        to = (z + d) % planes
        line_info(to).wait_send()
        line_back(to).wait_send()

    def finish(block, carry):
        for j in range(1, cols):
            spread(block, (k + j) % cols).wait_send()
            give_back(block, (k + j) % cols).wait_send()
        onward(block, lambda copy: copy.wait_send())
        forward(block).wait_send()
        half_back(block).wait_send()
        return carry

    lax.fori_loop(0, planes, finish, 0)


def expert_layer(inputs, info, hidden, up_weight, down_weight, planes, cols, cap):
    count, width = inputs.shape
    units = up_weight.shape[2]
    slots = cols * cap
    dma = pltpu.SemaphoreType.DMA
    bf16 = jnp.bfloat16
    vmem = pl.BlockSpec(memory_space=pltpu.VMEM)
    return pl.pallas_call(
        functools.partial(moe_kernel, planes, cols, cap),
        out_shape=jax.ShapeDtypeStruct((count, width), bf16),
        in_specs=[vmem, vmem, vmem, pl.BlockSpec(memory_space=pl.ANY), pl.BlockSpec(memory_space=pl.ANY)],
        out_specs=vmem,
        scratch_shapes=[
            pltpu.VMEM((units, width), bf16),
            pltpu.VMEM((units, width), bf16),
            pltpu.VMEM((planes, count, width), bf16),
            pltpu.VMEM((planes, 2 * count, slots), bf16),
            pltpu.VMEM((planes, slots, width), bf16),
            pltpu.VMEM((planes, 2, slots, width), bf16),
            pltpu.VMEM((2 * slots, units), bf16),
            pltpu.VMEM((planes, slots, width), bf16),
            pltpu.VMEM((planes, slots, width), bf16),
            pltpu.VMEM((planes, slots, width), bf16),
            pltpu.VMEM((planes, slots, width), bf16),
            pltpu.VMEM((planes, count, width), bf16),
            pltpu.VMEM((planes, count, width), bf16),
            pltpu.VMEM((2 * slots, units), jnp.float32),
            dma((2,)),
            dma((planes,)), dma((planes,)), dma((planes,)), dma((planes,)), dma((planes,)),
            dma((planes, cols)), dma((planes, cols)),
            dma((planes,)), dma((planes,)), dma((planes,)), dma((planes,)),
            dma((planes, cols)), dma((planes, cols)),
            dma((planes,)), dma((planes,)),
        ],
        compiler_params=pltpu.CompilerParams(
            collective_id=1, has_side_effects=True, vmem_limit_bytes=60 * 1024 * 1024
        ),
        cost_estimate=pl.CostEstimate(
            flops=8 * planes * slots * width * units,
            bytes_accessed=4 * width * units,
            transcendentals=0,
        ),
    )(inputs, info, hidden, up_weight.swapaxes(1, 2), down_weight)


def per_device(
    ssm_values,
    ssm_gate,
    write_proj,
    read_proj,
    step_size,
    decay_power,
    skip_gain,
    norm_gain,
    out_weight,
    residual,
    expert_norm,
    router_weight,
    expert_index,
    up_weight,
    down_weight,
):
    tokens_dev = ssm_values.shape[0]
    decay_rates = jnp.exp2(-decay_power.astype(jnp.float32))
    mixed_out = mixer(
        ssm_values, ssm_gate, write_proj, read_proj, step_size, decay_rates, skip_gain, norm_gain,
        out_weight,
    )
    rows_own = tokens_dev // lax.axis_size("head")
    hidden = residual.astype(jnp.float32) + mixed_out
    inputs = (
        hidden
        * lax.rsqrt(jnp.mean(hidden * hidden, axis=-1, keepdims=True) + EPSILON)
        * expert_norm[None, :]
    ).astype(jnp.bfloat16)
    logits = jnp.dot(inputs, router_weight, preferred_element_type=jnp.float32)
    experts = router_weight.shape[1]
    model_width = inputs.shape[1]
    expert_hits = expert_index[:, :, None] == jnp.arange(experts, dtype=jnp.int32)[None, None, :]
    picked = jnp.sum(jnp.where(expert_hits, logits[:, None, :], 0.0), axis=-1)
    probability = jax.nn.sigmoid(picked)
    shares = ROUTE_SCALE * probability / jnp.sum(probability, axis=1, keepdims=True)
    capacity = (
        8
        * TOP
        * tokens_dev
        // (3 * lax.axis_size("seq") * lax.axis_size("head") * lax.axis_size("head"))
    )
    flat_hits = expert_hits.astype(jnp.int32).reshape(rows_own * TOP, experts)
    before = jnp.cumsum(flat_hits, axis=0) - flat_hits
    slot_index = jnp.sum(before * flat_hits, axis=1)
    cols = lax.axis_size("head")
    planes = lax.axis_size("seq") // 2
    cap = -(-capacity // 16) * 16
    target = expert_index * cap + slot_index.reshape(rows_own, TOP)
    chosen = target[:, :, None] == jnp.arange(experts * cap, dtype=jnp.int32)[None, None, :]
    place = jnp.any(chosen, axis=1).astype(jnp.bfloat16)
    weigh = jnp.sum(jnp.where(chosen, shares[:, :, None], 0.0), axis=1).astype(jnp.bfloat16)
    info = jnp.concatenate([place, weigh], axis=0)
    info = info.reshape(2 * rows_own, planes, cols * cap).transpose(1, 0, 2)
    return expert_layer(inputs, info, hidden, up_weight, down_weight, planes, cols, cap)


def solution(mesh):
    return jax.shard_map(
        per_device,
        mesh=mesh,
        in_specs=(
            P(("grp", "seq"), "head"),
            P(("grp", "seq"), "head"),
            P(("grp", "seq"), "head"),
            P(("grp", "seq"), "head"),
            P(("grp", "seq"), "head"),
            P("head"),
            P("head"),
            P("head"),
            P("head", "seq"),
            P(("grp", "seq", "head"), None),
            P(),
            P(),
            P(("grp", "seq", "head"), None),
            P(("seq", "head"), None, None),
            P(("seq", "head"), None, None),
        ),
        out_specs=P(("grp", "seq", "head"), None),
        check_vma=False,
    )
```
